512 devices in a mesh: ctx: 16 (over x_lo, z), ch: 32 (over x_hi, y, core).
Axes of the slice: x: 4 (x_hi: 2, x_lo: 2; x = x_hi * 2 + x_lo), y: 8, z: 8, core: 2. Of those that a mesh axis runs over, the one named last changes fastest.
Arguments:
- tokens: bfloat16 [2048, 4096], P('ctx', 'ch'), may hold values from -6 to 6
- in_weight: bfloat16 [4096, 3, 4096], P(None, None, 'ch'), may hold values from -0.09375 to 0.09375
- filter_taps: float32 [2048, 4096], P('ctx', 'ch'), may hold values from -0.125 to 0.125
- grad_out: bfloat16 [2048, 4096], P('ctx', 'ch'), may hold values from -0.125 to 0.125
Outputs:
- weight_grad: float32 [4096, 3, 4096], P('ctx', None, 'ch')
- filter_grad: float32 [2048, 4096], P('ctx', 'ch')
The draws below stay inside these ranges and needn't reach their ends.
All inputs are finite; a program needn't handle non-finite values.
Results may differ from the reference program's by a relative error of at most 0.029.
Values may be sent and summed in bfloat16 or wider, within the bound.
A program may use at most 64 MiB of HBM per device.

```python
import jax
import jax.numpy as jnp
from jax import lax

D = 4096
C = 4096
L_DEV = 128
SEQ = 2048
N_CTX = 16


def strengthened(drawn, key, source, target, parts, factor):
    def block_of(dim):
        return (jnp.arange(drawn.shape[dim]) // (drawn.shape[dim] // parts)).reshape((-1,) + (1,) * (drawn.ndim - 1 - dim))

    first = jax.random.permutation(key, parts)[block_of(target)]
    other_side = (block_of(target) + parts // 2) % parts
    return jnp.where((block_of(source) == first) | (block_of(source) == other_side), factor * drawn, drawn)


def steps_of(own_key, dims, shards, smallest, top_value):
    level = 1.0
    for position, parts in shards:
        draws = jax.random.uniform(jax.random.fold_in(jax.random.fold_in(own_key, 6), position), (parts,), jnp.float32, smallest / len(shards), top_value / len(shards))
        level = level * jnp.repeat(jnp.exp(draws), dims[position] // parts).reshape((-1,) + (1,) * (len(dims) - 1 - position))
    return level


def bell_draw(stream_key, shape, width, bound, shards=(), held_as=jnp.bfloat16):
    array = width * jax.random.normal(stream_key, shape, jnp.float32)
    if shards:
        array = array * steps_of(stream_key, shape, shards, -0.22, 0.18)
    return jnp.clip(array, -bound, bound).astype(held_as)


def bell_draw_with(stream_key, extent, scale, bound, split, heavy, dtype=jnp.bfloat16):
    entries = scale * jax.random.normal(stream_key, extent, jnp.float32)
    if split:
        entries = entries * steps_of(stream_key, extent, split, -0.22, 0.18)
    return jnp.clip(strengthened(entries, jax.random.fold_in(stream_key, 3), *heavy), -bound, bound).astype(dtype)


def setup_inputs(seed: int = 0) -> dict:
    key_of = jax.random.split(jax.random.key(seed), 5)
    return {
        "tokens": bell_draw_with(key_of[0], (SEQ, D), 1.0, 6.0, ((0, 16), (1, 32)), (0, 1, 32, 2.75)),
        "in_weight": bell_draw(key_of[1], (D, 3, C), D ** -0.5, 0.09375, ((2, 32),)),
        "filter_taps": bell_draw(key_of[2], (SEQ, C), SEQ ** -0.5, 0.125, ((0, 16), (1, 32)), jnp.float32),
        "grad_out": bell_draw(key_of[3], (SEQ, C), SEQ ** -0.5, 0.125, ((0, 16), (1, 32))),
    }


def causal_spectrum(values):
    return jnp.fft.rfft(values, n=2 * SEQ, axis=0)


def back_to_time(spectrum):
    return jnp.fft.irfft(spectrum, n=2 * SEQ, axis=0)[:SEQ].astype(jnp.float32)


def reference(tokens, in_weight, filter_taps, grad_out):
    flat_weight = in_weight.reshape(D, 3 * C)
    proj = jnp.dot(tokens, flat_weight, preferred_element_type=jnp.float32).astype(jnp.bfloat16).reshape(SEQ, 3, C)
    query_proj = proj[:, 0].astype(jnp.float32)
    key_proj = proj[:, 1].astype(jnp.float32)
    value_proj = proj[:, 2].astype(jnp.float32)
    upstream = grad_out.astype(jnp.float32)
    product = key_proj * value_proj
    grad_z = upstream * query_proj
    filter_spec = causal_spectrum(filter_taps)
    product_spec = causal_spectrum(product)
    grad_spec = causal_spectrum(grad_z)
    conv_out = back_to_time(filter_spec * product_spec)
    grad_mix = back_to_time(jnp.conj(filter_spec) * grad_spec)
    filter_grad = back_to_time(grad_spec * jnp.conj(product_spec))
    grad_query = (upstream * conv_out).astype(jnp.bfloat16)
    grad_key = (grad_mix * value_proj).astype(jnp.bfloat16)
    grad_value = (grad_mix * key_proj).astype(jnp.bfloat16)
    grad_proj = jnp.stack([grad_query, grad_key, grad_value], axis=1).reshape(N_CTX, L_DEV, 3 * C)
    token_blocks = tokens.reshape(N_CTX, L_DEV, D)

    def add_block(running, block_pair):
        partial_term = jnp.dot(block_pair[0].T, block_pair[1], preferred_element_type=jnp.float32).astype(jnp.bfloat16)
        partial_term = lax.optimization_barrier(partial_term)
        return running + partial_term.astype(jnp.float32), None

    weight_grad, unused = lax.scan(add_block, jnp.zeros((D, 3 * C), jnp.float32), (token_blocks, grad_proj))
    return weight_grad.reshape(D, 3, C), filter_grad
```

```python
import math

import jax
import jax.numpy as jnp
import ml_dtypes
import numpy as np
from jax import lax
from jax.experimental import pallas as pl
from jax.experimental.pallas import tpu as pltpu
from jax.sharding import PartitionSpec as P

MESH = pl.DeviceIdType.MESH
BF16 = jnp.bfloat16
F32 = jnp.float32
ROWS = 128
TILES = 16
CHUNKS = 4


def transform_tables():
    r = np.arange(128)
    k1 = np.arange(128)
    forward = np.zeros((16, 256, 256))
    inverse = np.zeros((16, 256, 256))
    for k2 in range(1, 16):
        angle = 2 * np.pi * (((k2 + 32 * k1)[:, None] * r[None, :]) % 4096) / 4096
        c, s = np.cos(angle), np.sin(angle)
        forward[k2] = np.block([[c, s], [-s, c]])
        inverse[k2] = np.block([[c.T, -s.T], [s.T, c.T]]) * (2 / 4096)
    k1 = np.arange(64)
    a0 = 2 * np.pi * ((32 * k1[:, None] * r[None, :]) % 4096) / 4096
    a16 = 2 * np.pi * (((16 + 32 * k1)[:, None] * r[None, :]) % 4096) / 4096
    nyquist = 1.0 - 2.0 * (r % 2)
    re0, im0 = np.cos(a0), -np.sin(a0)
    im0[0] = nyquist
    zero = np.zeros((64, 128))
    forward[0] = np.block(
        [
            [re0, zero],
            [zero, np.cos(a16)],
            [im0, zero],
            [zero, -np.sin(a16)],
        ]
    )
    back_re0, back_im0 = 2 * np.cos(a0).T, -2 * np.sin(a0).T
    back_re0[:, 0] = 1.0
    back_im0[:, 0] = nyquist
    zero = np.zeros((128, 64))
    inverse[0] = (
        np.block(
            [
                [back_re0, zero, back_im0, zero],
                [zero, 2 * np.cos(a16).T, zero, -2 * np.sin(a16).T],
            ]
        )
        / 4096
    )
    block = np.arange(16)[:, None]
    k = np.arange(16)[None, :]
    angle = 2 * np.pi * ((block * k) % 32) / 32
    im_part = -np.sin(angle)
    im_part[:, 0] = 1.0 - 2.0 * (np.arange(16) % 2)
    single = np.concatenate([np.cos(angle), im_part], axis=1)
    single = np.broadcast_to(single[:, :, None], (16, 32, 128))
    return (
        forward.astype(ml_dtypes.bfloat16),
        inverse.astype(ml_dtypes.bfloat16),
        single.astype(np.float32),
    )


def root(n, a, sign):
    angle = -sign * 2 * math.pi * a / n
    return math.cos(angle), math.sin(angle)


def times(v, w):
    re, im = v
    wr, wi = w
    if abs(wi) < 1e-12:
        return (re, im) if wr > 0 else (-re, -im)
    if abs(wr) < 1e-12:
        return (-im, re) if wi > 0 else (im, -re)
    return re * wr - im * wi, re * wi + im * wr


def complex_dft(u, sign):
    n = len(u)
    if n == 1:
        return u
    h = n // 2
    low = [(u[a][0] + u[a + h][0], u[a][1] + u[a + h][1]) for a in range(h)]
    high = [
        times((u[a][0] - u[a + h][0], u[a][1] - u[a + h][1]), root(n, a, sign))
        for a in range(h)
    ]
    even, odd = complex_dft(low, sign), complex_dft(high, sign)
    return [even[i // 2] if i % 2 == 0 else odd[i // 2] for i in range(n)]


def real_forward(n, x):
    if n == 2:
        return [(x[0] + x[1], None), (x[0] - x[1], None)]
    h, q = n // 2, n // 4
    if len(x) == h:
        fold, diff = x, x
    else:
        fold = [x[a] + x[a + h] for a in range(h)]
        diff = [x[a] - x[a + h] for a in range(h)]
    even = real_forward(h, fold)
    odd = complex_dft(
        [times((diff[a], -diff[a + q]), root(n, a, 1)) for a in range(q)], 1
    )
    out = [None] * (h + 1)
    for m in range(h // 2 + 1):
        out[2 * m] = even[m]
    for j in range(q):
        k = 4 * j + 1
        if k <= h:
            out[k] = odd[j]
        else:
            out[n - k] = (odd[j][0], -odd[j][1])
    return out


def real_inverse(n, z, half=False):
    if n == 2:
        return [z[0][0] + z[1][0], z[0][0] - z[1][0]]
    h, q = n // 2, n // 4
    even = real_inverse(h, z[0::2])
    v = []
    for j in range(q):
        k = 4 * j + 1
        v.append(z[k] if k <= h else (z[n - k][0], -z[n - k][1]))
    s = complex_dft(v, -1)
    t = [times(s[a], root(n, a, -1)) for a in range(q)]
    odd = [t[a][0] for a in range(q)] + [-t[a][1] for a in range(q)]
    low = [even[a] + odd[a] for a in range(h)]
    return low if half else low + [even[a] - odd[a] for a in range(h)]


class Ring:
    def __init__(self, slot, half, place, right, left, send_sem, recv_sem):
        self.slot, self.half, self.place = slot, half, place
        self.to = (right, left)
        self.send_sem, self.recv_sem = send_sem, recv_sem

    def at(self, away):
        return lax.rem(self.place + 8 + away, 8)

    def copy(self, ref, way, step):
        return pltpu.make_async_remote_copy(
            src_ref=ref,
            dst_ref=ref,
            send_sem=self.send_sem.at[way, step - 1],
            recv_sem=self.recv_sem.at[way, step - 1],
            device_id=self.to[way],
            device_id_type=MESH,
        )

    def sent(self, way, step):
        away = (1 - step) if way == 0 else (step - 1)
        ref = self.slot(self.at(away))
        return self.copy(self.half(ref, way) if step == 4 else ref, way, step)

    def send(self, step):
        for way in range(2):
            self.sent(way, step).start()

    def wait(self, step):
        for way in range(2):
            ref = self.slot(self.at(-step if way == 0 else step))
            self.copy(self.half(ref, way) if step == 4 else ref, way, step).wait_recv()

    def drain(self):
        for step in range(1, 5):
            for way in range(2):
                self.sent(way, step).wait_send()


def half_of(rows):
    def half(ref, way):
        return ref.at[pl.ds(way * (rows // 2), rows // 2)]

    return half


def kernel(
    tok_ref, go_ref, taps_ref, w_hbm, f_hbm, g_hbm, ct_hbm,
    wg_ref, fg_ref,
    w_v, f_v, g_v, ct_v, tokb, gtb, gtx, qvb, qvx, tb, acc, bv, yb, fs, zb, gp,
    rown, rsend, rrecv, fown, fsend, frecv,
    local_sem, ra_s, ra_r, rb_s, rb_r, ga_s, ga_r, gb_s, gb_r, qa_s, qa_r, qb_s, qb_r,
    pair_s, pair_r, sib_s, sib_r, tr_s, tr_r, ty_s, ty_r, tx_s, tx_r, tx2_s, tx2_r, ts_s, ts_r,
):
    ctx, ch = lax.axis_index("ctx"), lax.axis_index("ch")
    xl, z = ctx // 8, lax.rem(ctx, 8)
    c, xh, y = lax.rem(ch, 2), ch // 16, lax.rem(ch // 2, 8)
    ox, oh, oc = 1 - xl, 1 - xh, 1 - c

    def dev(xh_, xl_, y_, z_, c_):
        return (xl_ * 8 + z_, (xh_ * 8 + y_) * 2 + c_)

    def remote(src, dst, s, r, to):
        return pltpu.make_async_remote_copy(
            src_ref=src, dst_ref=dst, send_sem=s, recv_sem=r, device_id=to, device_id_type=MESH
        )

    def turn(v, by):
        return lax.rem(v + 8 + by, 8)

    loads = [
        pltpu.make_async_copy(w_hbm, w_v, local_sem.at[0]),
        pltpu.make_async_copy(f_hbm, f_v, local_sem.at[1]),
        pltpu.make_async_copy(g_hbm, g_v, local_sem.at[2]),
        pltpu.make_async_copy(ct_hbm, ct_v, local_sem.at[3]),
    ]
    for load in loads:
        load.start()

    y_right, y_left = dev(xh, xl, turn(y, 1), z, c), dev(xh, xl, turn(y, -1), z, c)
    z_right, z_left = dev(xh, xl, y, turn(z, 1), c), dev(xh, xl, y, turn(z, -1), c)
    sibling = dev(xh, xl, y, z, oc)
    h_partner = dev(oh, xl, y, z, c)
    l_partner = dev(xh, ox, y, z, c)
    place = 2 * xh + xl
    x_up, x_down = lax.rem(place + 1, 4), lax.rem(place + 3, 4)
    x_right = dev(x_up // 2, lax.rem(x_up, 2), y, z, c)
    x_left = dev(x_down // 2, lax.rem(x_down, 2), y, z, c)

    barrier = pltpu.get_barrier_semaphore()
    peers = [y_right, y_left, sibling]
    peers += [dev(xh, xl, y, turn(z, by), c) for by in range(1, 8)]
    for by in range(1, 4):
        other = lax.rem(place + by, 4)
        peers.append(dev(other // 2, lax.rem(other, 2), y, z, c))
    for peer in peers:
        pl.semaphore_signal(barrier, inc=1, device_id=peer, device_id_type=MESH)

    own_tok = tok_ref[...]
    tokb[xh, y, c] = own_tok

    @pl.when(y == z)
    def _():
        tb[xh, c, xl, z] = own_tok

    lane = lax.broadcasted_iota(jnp.int32, (64, 128), 1)
    low64 = lane < 64
    low128 = lax.broadcasted_iota(jnp.int32, (128, 128), 1) < 64

    def flip(v):
        return pltpu.roll(v, 64, 1)

    def fold_low(v, h):
        top, bottom = v[:64], v[64:]
        return jnp.where(low64, top, flip(bottom)) if h == 0 else jnp.where(low64, flip(top), bottom)

    def fold_high(v, h):
        top, bottom = v[:64], v[64:]
        return jnp.where(low64, bottom, flip(top)) if h == 0 else jnp.where(low64, flip(bottom), top)

    go = go_ref[...].astype(F32)
    taps = taps_ref[...]
    packs = [
        jnp.concatenate([fold_high(go, h), fold_low(taps, h)], axis=0).astype(BF16)
        for h in range(2)
    ]
    first = xl == 0
    gtb[z, xl] = jnp.where(first, packs[0], packs[1])
    gtx[...] = jnp.where(first, packs[1], packs[0])

    pl.semaphore_wait(barrier, len(peers))

    ring_a = Ring(lambda q: tokb.at[xh, q, c], half_of(128), y, y_right, y_left, ra_s, ra_r)
    ring_b = Ring(lambda q: tokb.at[oh, q, c], half_of(128), y, y_right, y_left, rb_s, rb_r)
    gate_a = Ring(lambda q: gtb.at[q, xl], half_of(128), z, z_right, z_left, ga_s, ga_r)
    gate_b = Ring(lambda q: gtb.at[q, ox], half_of(128), z, z_right, z_left, gb_s, gb_r)
    proj_a = Ring(lambda q: qvb.at[q, xl], half_of(192), z, z_right, z_left, qa_s, qa_r)
    proj_b = Ring(lambda q: qvb.at[q, ox], half_of(192), z, z_right, z_left, qb_s, qb_r)

    def sib_copy(side, index, away, core):
        ref = tokb.at[xh if side == 0 else oh, turn(y, away), core]
        return remote(ref, ref, sib_s.at[side, index], sib_r.at[side, index], sibling)

    index_of = {0: 0, -1: 1, -2: 2, -3: 3, 4: 4, 1: 5, 2: 6, 3: 7}

    def to_sibling(side, aways):
        for away in aways:
            sib_copy(side, index_of[away], away, c).start()

    tok_pair_out = remote(tokb.at[xh, y, c], tokb.at[xh, y, c], pair_s.at[0], pair_r.at[0], h_partner)
    tok_pair_in = remote(tokb.at[oh, y, c], tokb.at[oh, y, c], pair_s.at[0], pair_r.at[0], h_partner)
    gate_out = remote(gtx, gtb.at[z, xl], pair_s.at[1], pair_r.at[1], l_partner)
    gate_in = remote(gtx, gtb.at[z, ox], pair_s.at[1], pair_r.at[1], l_partner)
    proj_out = remote(qvx, qvb.at[z, xl], pair_s.at[2], pair_r.at[2], l_partner)
    proj_in = remote(qvx, qvb.at[z, ox], pair_s.at[2], pair_r.at[2], l_partner)

    tok_pair_out.start()
    ring_a.send(1)
    to_sibling(0, [0])
    gate_out.start()
    gate_a.send(1)
    turn_own = tb.at[xh, c, xl, z]
    turn_out = remote(tokb.at[xh, y, c], turn_own, tr_s.at[0], tr_r.at[z], dev(xh, xl, y, y, c))

    @pl.when(y != z)
    def _():
        turn_out.start()

    tok_pair_in.wait_recv()
    ring_b.send(1)
    to_sibling(1, [0])
    gate_in.wait_recv()
    gate_b.send(1)
    acc[...] = jnp.zeros_like(acc)
    loads[0].wait()

    def project(away):
        for side in range(2):
            sib_copy(side, index_of[away], away, oc).wait_recv()
            q = turn(y, away)
            h = xh if side == 0 else oh
            left = jnp.concatenate([tokb[h, q, 0], tokb[h, q, 1]], axis=1)
            rows = pl.ds(pl.multiple_of((h * 8 + q) * 256, 256), 256)
            right = jnp.concatenate([w_v[j, rows, :] for j in range(3)], axis=1)
            acc[...] += jnp.dot(left, right, preferred_element_type=F32)

    for step in range(1, 5):
        new = [-step, step] if step < 4 else [4]
        for side, ring in ((0, ring_a), (1, ring_b)):
            ring.wait(step)
            if step < 4:
                ring.send(step + 1)
            to_sibling(side, new)
        for ring in (gate_a, gate_b):
            ring.wait(step)
            if step < 4:
                ring.send(step + 1)
        for away in [0] if step == 1 else [1 - step, step - 1]:
            project(away)
    project(4)

    projected = acc[...].astype(BF16).astype(F32)
    qp, kp, vp = projected[:, :128], projected[:, 128:256], projected[:, 256:]
    both = []
    for h in range(2):
        kq = jnp.where(low128, kp, flip(qp)) if h == 0 else jnp.where(low128, flip(kp), qp)
        both.append(jnp.concatenate([kq, fold_low(vp, h)], axis=0).astype(BF16))
    qvx[...] = jnp.where(first, both[1], both[0])
    proj_out.start()
    qvb[z, xl] = jnp.where(first, both[0], both[1])
    proj_a.send(1)


    d = turn(y, -z)
    dist = jnp.where(d <= 4, d, 8 - d)
    goes_right = d <= 3
    goes_left = jnp.logical_or(d == 0, d >= 6)
    up_h, up_l = x_up // 2, lax.rem(x_up, 2)
    down_h, down_l = x_down // 2, lax.rem(x_down, 2)

    def block_of(h, core, l, k):
        return tb.at[h, core, l, pl.ds(2 * k, 2)]

    def along_y(way, k):
        ref = block_of(xh, c, xl, k)
        return remote(ref, ref, ty_s.at[way, k], ty_r.at[k], y_right if way == 0 else y_left)

    def along_x(way, k):
        ref = block_of(xh, c, xl, k)
        return remote(ref, ref, tx_s.at[way, k], tx_r.at[way, k], x_right if way == 0 else x_left)

    def from_x(way, k):
        ref = block_of(down_h, c, down_l, k) if way == 0 else block_of(up_h, c, up_l, k)
        return remote(ref, ref, tx_s.at[way, k], tx_r.at[way, k], x_right if way == 0 else x_left)

    def half_on(way, k):
        h, l = (down_h, down_l) if way == 0 else (up_h, up_l)
        ref = tb.at[h, c, l, 2 * k + way]
        return remote(ref, ref, tx2_s.at[way, k], tx2_r.at[way, k], x_right if way == 0 else x_left)

    def half_from(way, k):
        ref = tb.at[oh, c, xl, 2 * k + way]
        return remote(ref, ref, tx2_s.at[way, k], tx2_r.at[way, k], x_right if way == 0 else x_left)

    piece_at = [(xh, xl), (down_h, down_l), (up_h, up_l), (oh, xl)]

    def t_sibling(piece, k, core):
        h, l = piece_at[piece]
        ref = block_of(h, core, l, k)
        return remote(ref, ref, ts_s.at[piece, k], ts_r.at[piece, k], sibling)

    def slot(tau):
        k = tau - dist

        @pl.when(jnp.logical_and(k >= 0, k < CHUNKS))
        def _():
            @pl.when(d != 0)
            def _():
                along_y(0, k).wait_recv()

            @pl.when(goes_right)
            def _():
                along_y(0, k).start()

            @pl.when(goes_left)
            def _():
                along_y(1, k).start()

            along_x(0, k).start()
            along_x(1, k).start()
            t_sibling(0, k, c).start()

        m = k - 1

        @pl.when(jnp.logical_and(m >= 0, m < CHUNKS))
        def _():
            from_x(0, m).wait_recv()
            half_on(0, m).start()
            from_x(1, m).wait_recv()
            half_on(1, m).start()
            t_sibling(1, m, c).start()
            t_sibling(2, m, c).start()

        n = k - 2

        @pl.when(jnp.logical_and(n >= 0, n < CHUNKS))
        def _():
            half_from(0, n).wait_recv()
            half_from(1, n).wait_recv()
            t_sibling(3, n, c).start()

    @pl.when(d == 0)
    def _():
        for by in range(1, 8):
            source = turn(z, by)
            ref = tb.at[xh, c, xl, source]
            remote(ref, ref, tr_s.at[0], tr_r.at[source], sibling).wait_recv()

    slot(0)
    proj_in.wait_recv()
    proj_b.send(1)


    def put_spectra(x, rows_lo, rows_hi):
        spectra = real_forward(32, x)
        yb[0, rows_lo, :] = spectra[0][0].astype(BF16)
        yb[0, rows_hi, :] = spectra[16][0].astype(BF16)
        for k in range(1, 16):
            yb[k, rows_lo, :] = spectra[k][0].astype(BF16)
            yb[k, rows_hi, :] = spectra[k][1].astype(BF16)

    low16 = lax.broadcasted_iota(jnp.int32, (16, 128), 1) < 64

    def rows_at(start):
        return pl.ds(pl.multiple_of(start, 16), 16)

    def filter_rows(i, carry):
        top, bottom = [], []
        for a in range(16):
            packed = gtb[a % 8, a // 8, rows_at(64 + 16 * i), :].astype(F32)
            turned = flip(packed)
            top.append(jnp.where(low16, packed, turned))
            bottom.append(jnp.where(low16, turned, packed))
        put_spectra(top, rows_at(16 * i), rows_at(128 + 16 * i))
        put_spectra(bottom, rows_at(64 + 16 * i), rows_at(192 + 16 * i))
        return carry

    lax.fori_loop(0, 4, filter_rows, 0)
    loads[1].wait()
    row0 = lax.broadcasted_iota(jnp.int32, (128, 128), 0) == 0

    def filter_tile(k, carry):
        spec = jnp.dot(f_v[k], yb[k], preferred_element_type=F32)
        fs[k, :128, :] = spec[:128]
        im = spec[128:]
        special = jnp.logical_and(row0, k == 0)
        fs[k, 128:, :] = jnp.where(jnp.logical_or(low128, special), im, -im)
        return carry

    lax.fori_loop(0, 16, filter_tile, 0)

    for step in range(1, 5):
        for ring in (proj_a, proj_b):
            ring.wait(step)
            if step < 4:
                ring.send(step + 1)
        slot(step)


    def field_rows(i, carry):
        top, bottom = [], []
        for a in range(16):
            za, la = a % 8, a // 8
            vals = qvb[za, la, rows_at(128 + 16 * i), :].astype(F32)
            gos = gtb[za, la, rows_at(16 * i), :].astype(F32)
            b_top = jnp.where(low16, vals, gos)
            b_bottom = flip(jnp.where(low16, gos, vals))
            bv[a, rows_at(16 * i), :] = b_top.astype(BF16)
            bv[a, rows_at(64 + 16 * i), :] = b_bottom.astype(BF16)
            top.append(qvb[za, la, rows_at(16 * i), :].astype(F32) * b_top)
            bottom.append(qvb[za, la, rows_at(64 + 16 * i), :].astype(F32) * b_bottom)
        put_spectra(top, rows_at(16 * i), rows_at(128 + 16 * i))
        put_spectra(bottom, rows_at(64 + 16 * i), rows_at(192 + 16 * i))
        return carry

    lax.fori_loop(0, 4, field_rows, 0)
    slot(5)
    loads[2].wait()

    def mix_tile(k, carry):
        spec = jnp.dot(f_v[k], yb[k], preferred_element_type=F32)
        sr, si = spec[:128], spec[128:]
        fr, fi = fs[k, :128, :], fs[k, 128:, :]
        tr, ti = flip(sr), flip(si)
        special = jnp.logical_and(row0, k == 0)
        mixed_re = jnp.where(special, fr * sr, fr * sr - fi * si)
        mixed_im = jnp.where(special, fi * si, fr * si + fi * sr)
        grad_re = jnp.where(special, tr * sr, tr * sr + ti * si)
        grad_im = jnp.where(special, ti * si, ti * sr - tr * si)
        mixed = jnp.concatenate(
            [
                jnp.concatenate([mixed_re, grad_re], axis=1),
                jnp.concatenate([mixed_im, grad_im], axis=1),
            ],
            axis=0,
        ).astype(BF16)
        zb[k] = jnp.dot(g_v[k], mixed, preferred_element_type=F32)
        return carry

    lax.fori_loop(0, 16, mix_tile, 0)
    slot(6)


    def back_rows(i, carry):
        lo, hi = rows_at(16 * i), rows_at(128 + 16 * i)
        spectra = [(zb[0, lo, :128], None)]
        spectra += [(zb[k, lo, :128], zb[k, hi, :128]) for k in range(1, 16)]
        spectra += [(zb[0, hi, :128], None)]
        for a, restored in enumerate(real_inverse(32, spectra, half=True)):
            turned = flip(restored)
            out = rows_at(128 * a + 16 * i)
            gp[out, :128] = (turned * bv[a, lo, :].astype(F32)).astype(BF16)
            gp[out, 128:] = (turned * qvb[a % 8, a // 8, lo, :].astype(F32)).astype(BF16)
        return carry

    lax.fori_loop(0, 8, back_rows, 0)
    slot(7)
    slot(8)
    slot(9)


    for piece in range(4):
        for k in range(CHUNKS):
            t_sibling(piece, k, oc).wait_recv()

    def weight_rows(h, core):
        lhs = tb[h, core].reshape(2048, 128)
        return lax.dot_general(lhs, gp[...], (((0,), (0,)), ((), ())), preferred_element_type=F32)

    away_parts = [weight_rows(ox, core) for core in range(2)]
    for core in range(2):
        rsend[core * 128 : core * 128 + 128, :] = away_parts[core][:, :128].astype(BF16)
    rsend[256:, :] = jnp.where(low128, away_parts[0][:, 128:], flip(away_parts[1][:, 128:])).astype(BF16)
    weight_out = remote(rsend, rrecv, pair_s.at[3], pair_r.at[3], l_partner)
    weight_out.start()

    loads[3].wait()

    def filter_grad_step(k, carry):
        sums = []
        for l in range(2):
            block = z + 8 * l
            total = carry[l] + ct_v[block, pl.ds(k, 1), :] * zb[k, :128, 128:]
            sums.append(total + ct_v[block, pl.ds(k + 16, 1), :] * zb[k, 128:, 128:])
        return tuple(sums)

    zero = jnp.zeros((128, 128), F32)
    near, far = lax.fori_loop(0, 16, filter_grad_step, (zero, zero))
    own = jnp.where(first, near, far)
    other = jnp.where(first, far, near)
    fsend[...] = jnp.where(low64, other[:64], flip(other[64:]))
    filter_out = remote(fsend, frecv, pair_s.at[4], pair_r.at[4], l_partner)
    filter_out.start()
    fown[...] = own

    for core in range(2):
        rown[core * 128 : core * 128 + 128, :] = weight_rows(xl, core)

    def unfolded(mine, got):
        turned, turned_mine = flip(got), flip(mine)
        low = lax.broadcasted_iota(jnp.int32, mine.shape, 1) < 64
        as_first = jnp.where(low, mine, jnp.concatenate([turned, got], axis=0))
        as_second = jnp.where(low, jnp.concatenate([got, turned], axis=0), turned_mine)
        return jnp.where(first, as_first, as_second)

    weight_out.wait_recv()
    mine = rown[:, :128]
    got = rrecv[:256, :].astype(F32)
    mine_turned, got_turned = flip(mine), flip(got)
    low256 = lax.broadcasted_iota(jnp.int32, (256, 128), 1) < 64
    wg_ref[0] = jnp.where(
        first, jnp.where(low256, mine_turned, got), jnp.where(low256, got_turned, mine)
    )
    wg_ref[1] = jnp.where(
        first, jnp.where(low256, mine, got_turned), jnp.where(low256, got, mine_turned)
    )
    wg_ref[2] = unfolded(rown[:, 128:], rrecv[256:, :].astype(F32))
    filter_out.wait_recv()
    fg_ref[...] = unfolded(fown[...], frecv[...])

    for ring in (ring_a, ring_b, gate_a, gate_b, proj_a, proj_b):
        ring.drain()
    for sent in (tok_pair_out, gate_out, proj_out, weight_out, filter_out):
        sent.wait_send()
    for side in range(2):
        for away, index in index_of.items():
            sib_copy(side, index, away, c).wait_send()

    @pl.when(y != z)
    def _():
        turn_out.wait_send()

    for k in range(CHUNKS):

        @pl.when(goes_right)
        def _():
            along_y(0, k).wait_send()

        @pl.when(goes_left)
        def _():
            along_y(1, k).wait_send()

        for way in range(2):
            along_x(way, k).wait_send()
            half_on(way, k).wait_send()
        for piece in range(4):
            t_sibling(piece, k, c).wait_send()


def on_device(tables, tokens, in_weight, filter_taps, grad_out):
    forward, inverse, single = tables
    vmem = pl.BlockSpec(memory_space=pltpu.VMEM)
    anywhere = pl.BlockSpec(memory_space=pl.ANY)
    dma = pltpu.SemaphoreType.DMA
    ring_sems = [dma((2, 4)) for _ in range(12)]
    weight_grad, filter_grad = pl.pallas_call(
        kernel,
        out_shape=(
            jax.ShapeDtypeStruct((3, 256, 128), F32),
            jax.ShapeDtypeStruct((128, 128), F32),
        ),
        in_specs=[vmem] * 3 + [anywhere] * 4,
        out_specs=(vmem, vmem),
        scratch_shapes=[
            pltpu.VMEM((3, 4096, 128), BF16),
            pltpu.VMEM((16, 256, 256), BF16),
            pltpu.VMEM((16, 256, 256), BF16),
            pltpu.VMEM((16, 32, 128), F32),
            pltpu.VMEM((2, 8, 2, 128, 128), BF16),
            pltpu.VMEM((8, 2, 128, 128), BF16),
            pltpu.VMEM((128, 128), BF16),
            pltpu.VMEM((8, 2, 192, 128), BF16),
            pltpu.VMEM((192, 128), BF16),
            pltpu.VMEM((2, 2, 2, 8, 128, 128), BF16),
            pltpu.VMEM((128, 384), F32),
            pltpu.VMEM((16, 128, 128), BF16),
            pltpu.VMEM((16, 256, 128), BF16),
            pltpu.VMEM((16, 256, 128), F32),
            pltpu.VMEM((16, 256, 256), F32),
            pltpu.VMEM((2048, 256), BF16),
            pltpu.VMEM((256, 256), F32),
            pltpu.VMEM((384, 128), BF16),
            pltpu.VMEM((384, 128), BF16),
            pltpu.VMEM((128, 128), F32),
            pltpu.VMEM((64, 128), F32),
            pltpu.VMEM((64, 128), F32),
            dma((4,)),
            *ring_sems,
            dma((5,)), dma((5,)),
            dma((2, 8)), dma((2, 8)),
            dma((1,)), dma((8,)),
            dma((2, CHUNKS)), dma((CHUNKS,)),
            dma((2, CHUNKS)), dma((2, CHUNKS)),
            dma((2, CHUNKS)), dma((2, CHUNKS)),
            dma((4, CHUNKS)), dma((4, CHUNKS)),
        ],
        compiler_params=pltpu.CompilerParams(
            collective_id=0, has_side_effects=True, vmem_limit_bytes=52 * 1024 * 1024
        ),
        cost_estimate=pl.CostEstimate(flops=3_000_000_000, bytes_accessed=10_000_000, transcendentals=0),
    )(
        tokens,
        grad_out,
        filter_taps,
        jnp.transpose(in_weight, (1, 0, 2)),
        forward,
        inverse,
        single,
    )
    return jnp.transpose(weight_grad, (1, 0, 2)), filter_grad


def solution(mesh):
    tables = transform_tables()

    def whole(tokens, in_weight, filter_taps, grad_out):
        constants = tuple(jnp.asarray(t) for t in tables)
        placed = (P("ctx", "ch"), P(None, None, "ch"), P("ctx", "ch"), P("ctx", "ch"))
        return jax.shard_map(
            on_device,
            mesh=mesh,
            in_specs=((P(), P(), P()),) + placed,
            out_specs=(P("ctx", None, "ch"), P("ctx", "ch")),
            check_vma=False,
        )(constants, tokens, in_weight, filter_taps, grad_out)

    return whole
```

```python
import math

import jax
import jax.numpy as jnp
import ml_dtypes
import numpy as np
from jax import lax
from jax.experimental import pallas as pl
from jax.experimental.pallas import tpu as pltpu
from jax.sharding import PartitionSpec as P

MESH = pl.DeviceIdType.MESH
BF16 = jnp.bfloat16
F32 = jnp.float32
ROWS = 128
TILES = 16
CHUNKS = 2
PER = 8 // CHUNKS


def transform_tables():
    r = np.arange(128)
    k1 = np.arange(128)
    forward = np.zeros((16, 256, 256))
    inverse = np.zeros((16, 256, 256))
    for k2 in range(1, 16):
        angle = 2 * np.pi * (((k2 + 32 * k1)[:, None] * r[None, :]) % 4096) / 4096
        c, s = np.cos(angle), np.sin(angle)
        forward[k2] = np.block([[c, s], [-s, c]])
        inverse[k2] = np.block([[c.T, -s.T], [s.T, c.T]]) * (2 / 4096)
    k1 = np.arange(64)
    a0 = 2 * np.pi * ((32 * k1[:, None] * r[None, :]) % 4096) / 4096
    a16 = 2 * np.pi * (((16 + 32 * k1)[:, None] * r[None, :]) % 4096) / 4096
    nyquist = 1.0 - 2.0 * (r % 2)
    re0, im0 = np.cos(a0), -np.sin(a0)
    im0[0] = nyquist
    zero = np.zeros((64, 128))
    forward[0] = np.block(
        [
            [re0, zero],
            [zero, np.cos(a16)],
            [im0, zero],
            [zero, -np.sin(a16)],
        ]
    )
    back_re0, back_im0 = 2 * np.cos(a0).T, -2 * np.sin(a0).T
    back_re0[:, 0] = 1.0
    back_im0[:, 0] = nyquist
    zero = np.zeros((128, 64))
    inverse[0] = (
        np.block(
            [
                [back_re0, zero, back_im0, zero],
                [zero, 2 * np.cos(a16).T, zero, -2 * np.sin(a16).T],
            ]
        )
        / 4096
    )
    block = np.arange(16)[:, None]
    k = np.arange(16)[None, :]
    angle = 2 * np.pi * ((block * k) % 32) / 32
    im_part = -np.sin(angle)
    im_part[:, 0] = 1.0 - 2.0 * (np.arange(16) % 2)
    single = np.concatenate([np.cos(angle), im_part], axis=1)
    single = np.broadcast_to(single[:, :, None], (16, 32, 128))
    return (
        forward.astype(ml_dtypes.bfloat16),
        inverse.astype(ml_dtypes.bfloat16),
        single.astype(np.float32),
    )


def root(n, a, sign):
    angle = -sign * 2 * math.pi * a / n
    return math.cos(angle), math.sin(angle)


def times(v, w):
    re, im = v
    wr, wi = w
    if abs(wi) < 1e-12:
        return (re, im) if wr > 0 else (-re, -im)
    if abs(wr) < 1e-12:
        return (-im, re) if wi > 0 else (im, -re)
    return re * wr - im * wi, re * wi + im * wr


def complex_dft(u, sign):
    n = len(u)
    if n == 1:
        return u
    h = n // 2
    low = [(u[a][0] + u[a + h][0], u[a][1] + u[a + h][1]) for a in range(h)]
    high = [
        times((u[a][0] - u[a + h][0], u[a][1] - u[a + h][1]), root(n, a, sign))
        for a in range(h)
    ]
    even, odd = complex_dft(low, sign), complex_dft(high, sign)
    return [even[i // 2] if i % 2 == 0 else odd[i // 2] for i in range(n)]


def real_forward(n, x):
    if n == 2:
        return [(x[0] + x[1], None), (x[0] - x[1], None)]
    h, q = n // 2, n // 4
    if len(x) == h:
        fold, diff = x, x
    else:
        fold = [x[a] + x[a + h] for a in range(h)]
        diff = [x[a] - x[a + h] for a in range(h)]
    even = real_forward(h, fold)
    odd = complex_dft(
        [times((diff[a], -diff[a + q]), root(n, a, 1)) for a in range(q)], 1
    )
    out = [None] * (h + 1)
    for m in range(h // 2 + 1):
        out[2 * m] = even[m]
    for j in range(q):
        k = 4 * j + 1
        if k <= h:
            out[k] = odd[j]
        else:
            out[n - k] = (odd[j][0], -odd[j][1])
    return out


def real_inverse(n, z, half=False):
    if n == 2:
        return [z[0][0] + z[1][0], z[0][0] - z[1][0]]
    h, q = n // 2, n // 4
    even = real_inverse(h, z[0::2])
    v = []
    for j in range(q):
        k = 4 * j + 1
        v.append(z[k] if k <= h else (z[n - k][0], -z[n - k][1]))
    s = complex_dft(v, -1)
    t = [times(s[a], root(n, a, -1)) for a in range(q)]
    odd = [t[a][0] for a in range(q)] + [-t[a][1] for a in range(q)]
    low = [even[a] + odd[a] for a in range(h)]
    return low if half else low + [even[a] - odd[a] for a in range(h)]


class Spread:
    NAMES = {(-1, None): 0, (-2, None): 1, (-3, None): 2, (-4, 0): 3, (-4, 1): 4, (3, None): 5, (2, None): 6, (1, None): 7}

    def __init__(self, slot, rows, place, to, send_sem, recv_sem):
        self.slot, self.rows, self.place, self.to = slot, rows, place, to
        self.send_sem, self.recv_sem = send_sem, recv_sem
        self.sent = []

    def copy(self, ref, name, device):
        if name[1] is not None:
            ref = ref.at[pl.ds(name[1] * (self.rows // 2), self.rows // 2)]
        at = self.NAMES[name]
        return pltpu.make_async_remote_copy(
            src_ref=ref, dst_ref=ref, send_sem=self.send_sem.at[at], recv_sem=self.recv_sem.at[at],
            device_id=device, device_id_type=MESH,
        )

    def send(self, origin, distance, half=None):
        seen = origin - distance
        name = (-4 if seen == 4 else seen, half)
        copy = self.copy(self.slot(lax.rem(self.place + 8 + origin, 8)), name, self.to(distance))
        copy.start()
        self.sent.append(copy)

    def wait(self, origin, half=None):
        self.copy(self.slot(lax.rem(self.place + 8 + origin, 8)), (origin, half), self.to(1)).wait_recv()

    def first(self):
        for distance in (2, -2, 1, -1):
            self.send(0, distance)

    def middle(self):
        self.wait(-2)
        self.send(-2, 2, 0)
        self.send(-2, 1)
        self.wait(2)
        self.send(2, -2, 1)
        self.send(2, -1)
        self.wait(-1)
        self.wait(1)

    def last(self):
        self.wait(-3)
        self.wait(3)
        self.wait(-4, 0)
        self.wait(-4, 1)

    def drain(self):
        for copy in self.sent:
            copy.wait_send()


def kernel(
    tok_hbm, go_hbm, taps_hbm, w_hbm, f_hbm, g_hbm, ct_hbm,
    wg_ref, fg_ref,
    go_v, taps_v, w_v, f_v, g_v, ct_v, tokb, gtb, gtx, qvb, qvx, tb, acc, bv, yb, fs, zb, gp,
    rown, rsend, rrecv, fown, fsend, frecv,
    local_sem, ra_s, ra_r, rb_s, rb_r, ga_s, ga_r, gb_s, gb_r, qa_s, qa_r, qb_s, qb_r,
    pair_s, pair_r, sib_s, sib_r, tr_s, tr_r, tx_s, tx_r, tx2_s, tx2_r, ts_s, ts_r,
):
    ctx, ch = lax.axis_index("ctx"), lax.axis_index("ch")
    xl, z = ctx // 8, lax.rem(ctx, 8)
    c, xh, y = lax.rem(ch, 2), ch // 16, lax.rem(ch // 2, 8)
    ox, oh, oc = 1 - xl, 1 - xh, 1 - c

    def dev(xh_, xl_, y_, z_, c_):
        return (xl_ * 8 + z_, (xh_ * 8 + y_) * 2 + c_)

    def remote(src, dst, s, r, to):
        return pltpu.make_async_remote_copy(
            src_ref=src, dst_ref=dst, send_sem=s, recv_sem=r, device_id=to, device_id_type=MESH
        )

    def turn(v, by):
        return lax.rem(v + 8 + by, 8)

    def along(axis):
        if axis == "y":
            return lambda by: dev(xh, xl, turn(y, by), z, c)
        return lambda by: dev(xh, xl, y, turn(z, by), c)

    sibling = dev(xh, xl, y, z, oc)
    h_partner = dev(oh, xl, y, z, c)
    l_partner = dev(xh, ox, y, z, c)
    place = 2 * xh + xl
    x_up, x_down = lax.rem(place + 1, 4), lax.rem(place + 3, 4)
    x_right = dev(x_up // 2, lax.rem(x_up, 2), y, z, c)
    x_left = dev(x_down // 2, lax.rem(x_down, 2), y, z, c)

    barrier = pltpu.get_barrier_semaphore()
    peers = [sibling] + [along("y")(by) for by in (-2, -1, 1, 2)]
    peers += [along("z")(by) for by in range(1, 8)]
    for by in range(1, 4):
        other = lax.rem(place + by, 4)
        peers.append(dev(other // 2, lax.rem(other, 2), y, z, c))
    for peer in peers:
        pl.semaphore_signal(barrier, inc=1, device_id=peer, device_id_type=MESH)

    own_loads = [
        pltpu.make_async_copy(go_hbm, go_v, local_sem.at[4]),
        pltpu.make_async_copy(taps_hbm, taps_v, local_sem.at[5]),
        pltpu.make_async_copy(tok_hbm, tokb.at[xh, y, c], local_sem.at[6]),
    ]
    for load in own_loads:
        load.start()
    loads = [
        pltpu.make_async_copy(w_hbm, w_v, local_sem.at[0]),
        pltpu.make_async_copy(f_hbm, f_v, local_sem.at[1]),
        pltpu.make_async_copy(g_hbm, g_v, local_sem.at[2]),
        pltpu.make_async_copy(ct_hbm, ct_v, local_sem.at[3]),
    ]
    for load in loads:
        load.start()

    lane = lax.broadcasted_iota(jnp.int32, (64, 128), 1)
    low64 = lane < 64
    low128 = lax.broadcasted_iota(jnp.int32, (128, 128), 1) < 64

    def flip(v):
        return pltpu.roll(v, 64, 1)

    def fold_low(v, h):
        top, bottom = v[:64], v[64:]
        return jnp.where(low64, top, flip(bottom)) if h == 0 else jnp.where(low64, flip(top), bottom)

    def fold_high(v, h):
        top, bottom = v[:64], v[64:]
        return jnp.where(low64, bottom, flip(top)) if h == 0 else jnp.where(low64, flip(bottom), top)

    for load in own_loads:
        load.wait()
    go = go_v[...].astype(F32)
    taps = taps_v[...]
    packs = [
        jnp.concatenate([fold_high(go, h), fold_low(taps, h)], axis=0).astype(BF16)
        for h in range(2)
    ]
    first = xl == 0
    gtb[z, xl] = jnp.where(first, packs[0], packs[1])
    gtx[...] = jnp.where(first, packs[1], packs[0])

    pl.semaphore_wait(barrier, len(peers))

    tok_a = Spread(lambda q: tokb.at[xh, q, c], 128, y, along("y"), ra_s, ra_r)
    tok_b = Spread(lambda q: tokb.at[oh, q, c], 128, y, along("y"), rb_s, rb_r)
    gate_a = Spread(lambda q: gtb.at[q, xl], 128, z, along("z"), ga_s, ga_r)
    gate_b = Spread(lambda q: gtb.at[q, ox], 128, z, along("z"), gb_s, gb_r)
    proj_a = Spread(lambda q: qvb.at[q, xl], 192, z, along("z"), qa_s, qa_r)
    proj_b = Spread(lambda q: qvb.at[q, ox], 192, z, along("z"), qb_s, qb_r)

    def sib_copy(side, index, away, core):
        ref = tokb.at[xh if side == 0 else oh, turn(y, away), core]
        return remote(ref, ref, sib_s.at[side, index], sib_r.at[side, index], sibling)

    index_of = {0: 0, -1: 1, -2: 2, -3: 3, -4: 4, 3: 5, 2: 6, 1: 7}

    def to_sibling(side, aways):
        for away in aways:
            sib_copy(side, index_of[away], away, c).start()

    tok_pair_out = remote(tokb.at[xh, y, c], tokb.at[xh, y, c], pair_s.at[0], pair_r.at[0], h_partner)
    tok_pair_in = remote(tokb.at[oh, y, c], tokb.at[oh, y, c], pair_s.at[0], pair_r.at[0], h_partner)
    gate_out = remote(gtx, gtb.at[z, xl], pair_s.at[1], pair_r.at[1], l_partner)
    gate_in = remote(gtx, gtb.at[z, ox], pair_s.at[1], pair_r.at[1], l_partner)
    proj_out = remote(qvx, qvb.at[z, xl], pair_s.at[2], pair_r.at[2], l_partner)
    proj_in = remote(qvx, qvb.at[z, ox], pair_s.at[2], pair_r.at[2], l_partner)

    def turn_copy(away):
        q = turn(y, away)
        return remote(
            tokb.at[xh, q, c], tb.at[xh, c, xl, z], tr_s.at[index_of[away]], tr_r.at[z], dev(xh, xl, y, q, c)
        )

    def turned_over(aways):
        for away in aways:
            q = turn(y, away)

            @pl.when(q == z)
            def _():
                tb[xh, c, xl, z] = tokb[xh, q, c]

            @pl.when(q != z)
            def _():
                turn_copy(away).start()

    def project(aways):
        total = None
        for away in aways:
            for side in range(2):
                sib_copy(side, index_of[away], away, oc).wait_recv()
                q = turn(y, away)
                h = xh if side == 0 else oh
                left = jnp.concatenate([tokb[h, q, 0], tokb[h, q, 1]], axis=1)
                rows = pl.ds(pl.multiple_of((h * 8 + q) * 256, 256), 256)
                right = jnp.concatenate([w_v[j, rows, :] for j in range(3)], axis=1)
                term = jnp.dot(left, right, preferred_element_type=F32)
                total = term if total is None else total + term
        return total

    tok_pair_out.start()
    tok_a.first()
    to_sibling(0, [0])
    gate_out.start()
    gate_a.first()
    turned_over([0])
    tok_pair_in.wait_recv()
    tok_b.first()
    to_sibling(1, [0])
    gate_in.wait_recv()
    gate_b.first()
    loads[0].wait()
    near, far = [-2, 2, -1, 1], [-3, 3, -4]
    tok_a.middle()
    to_sibling(0, near)
    turned_over(near)
    acc[...] = project([0])
    tok_b.middle()
    to_sibling(1, near)
    gate_a.middle()
    gate_b.middle()
    tok_a.last()
    to_sibling(0, far)
    turned_over(far)
    acc[...] += project(near)
    tok_b.last()
    to_sibling(1, far)
    projected = (acc[...] + project(far)).astype(BF16).astype(F32)

    qp, kp, vp = projected[:, :128], projected[:, 128:256], projected[:, 256:]
    both = []
    for h in range(2):
        kq = jnp.where(low128, kp, flip(qp)) if h == 0 else jnp.where(low128, flip(kp), qp)
        both.append(jnp.concatenate([kq, fold_low(vp, h)], axis=0).astype(BF16))
    qvx[...] = jnp.where(first, both[1], both[0])
    proj_out.start()
    qvb[z, xl] = jnp.where(first, both[0], both[1])
    proj_a.first()


    up_h, up_l = x_up // 2, lax.rem(x_up, 2)
    down_h, down_l = x_down // 2, lax.rem(x_down, 2)

    def block_of(h, core, l, k):
        return tb.at[h, core, l, pl.ds(PER * k, PER)]

    def along_x(way, k):
        ref = block_of(xh, c, xl, k)
        return remote(ref, ref, tx_s.at[way, k], tx_r.at[way, k], x_right if way == 0 else x_left)

    def from_x(way, k):
        ref = block_of(down_h, c, down_l, k) if way == 0 else block_of(up_h, c, up_l, k)
        return remote(ref, ref, tx_s.at[way, k], tx_r.at[way, k], x_right if way == 0 else x_left)

    def half_on(way, k):
        h, l = (down_h, down_l) if way == 0 else (up_h, up_l)
        ref = tb.at[h, c, l, pl.ds(PER * k + PER // 2 * way, PER // 2)]
        return remote(ref, ref, tx2_s.at[way, k], tx2_r.at[way, k], x_right if way == 0 else x_left)

    def half_from(way, k):
        ref = tb.at[oh, c, xl, pl.ds(PER * k + PER // 2 * way, PER // 2)]
        return remote(ref, ref, tx2_s.at[way, k], tx2_r.at[way, k], x_right if way == 0 else x_left)

    piece_at = [(xh, xl), (down_h, down_l), (up_h, up_l), (oh, xl)]

    def t_sibling(piece, k, core):
        h, l = piece_at[piece]
        ref = block_of(h, core, l, k)
        return remote(ref, ref, ts_s.at[piece, k], ts_r.at[piece, k], sibling)

    def round_x_first():
        for k in range(CHUNKS):
            for source in range(PER * k, PER * k + PER):
                ref = tb.at[xh, c, xl, source]

                @pl.when(z != source)
                def _():
                    remote(ref, ref, tr_s.at[0], tr_r.at[source], sibling).wait_recv()

            along_x(0, k).start()
            along_x(1, k).start()
            t_sibling(0, k, c).start()

    def round_x_second():
        for k in range(CHUNKS):
            from_x(0, k).wait_recv()
            half_on(0, k).start()
            from_x(1, k).wait_recv()
            half_on(1, k).start()
            t_sibling(1, k, c).start()
            t_sibling(2, k, c).start()

    def round_x_third():
        for k in range(CHUNKS):
            half_from(0, k).wait_recv()
            half_from(1, k).wait_recv()
            t_sibling(3, k, c).start()

    round_x_first()
    proj_in.wait_recv()
    proj_b.first()
    gate_a.last()
    gate_b.last()


    def put_spectra(x, rows_lo, rows_hi):
        spectra = real_forward(32, x)
        yb[0, rows_lo, :] = spectra[0][0].astype(BF16)
        yb[0, rows_hi, :] = spectra[16][0].astype(BF16)
        for k in range(1, 16):
            yb[k, rows_lo, :] = spectra[k][0].astype(BF16)
            yb[k, rows_hi, :] = spectra[k][1].astype(BF16)

    low16 = lax.broadcasted_iota(jnp.int32, (16, 128), 1) < 64

    def rows_at(start):
        return pl.ds(pl.multiple_of(start, 16), 16)

    def filter_rows(i, carry):
        top, bottom = [], []
        for a in range(16):
            packed = gtb[a % 8, a // 8, rows_at(64 + 16 * i), :].astype(F32)
            turned = flip(packed)
            top.append(jnp.where(low16, packed, turned))
            bottom.append(jnp.where(low16, turned, packed))
        put_spectra(top, rows_at(16 * i), rows_at(128 + 16 * i))
        put_spectra(bottom, rows_at(64 + 16 * i), rows_at(192 + 16 * i))
        return carry

    lax.fori_loop(0, 4, filter_rows, 0)
    loads[1].wait()
    row0 = lax.broadcasted_iota(jnp.int32, (128, 128), 0) == 0

    def filter_tile(k, carry):
        spec = jnp.dot(f_v[k], yb[k], preferred_element_type=F32)
        fs[k, :128, :] = spec[:128]
        im = spec[128:]
        special = jnp.logical_and(row0, k == 0)
        fs[k, 128:, :] = jnp.where(jnp.logical_or(low128, special), im, -im)
        return carry

    lax.fori_loop(0, 16, filter_tile, 0, unroll=16)

    proj_a.middle()
    proj_b.middle()
    round_x_second()
    proj_a.last()
    proj_b.last()


    def field_rows(i, carry):
        top, bottom = [], []
        for a in range(16):
            za, la = a % 8, a // 8
            vals = qvb[za, la, rows_at(128 + 16 * i), :].astype(F32)
            gos = gtb[za, la, rows_at(16 * i), :].astype(F32)
            b_top = jnp.where(low16, vals, gos)
            b_bottom = flip(jnp.where(low16, gos, vals))
            bv[a, rows_at(16 * i), :] = b_top.astype(BF16)
            bv[a, rows_at(64 + 16 * i), :] = b_bottom.astype(BF16)
            top.append(qvb[za, la, rows_at(16 * i), :].astype(F32) * b_top)
            bottom.append(qvb[za, la, rows_at(64 + 16 * i), :].astype(F32) * b_bottom)
        put_spectra(top, rows_at(16 * i), rows_at(128 + 16 * i))
        put_spectra(bottom, rows_at(64 + 16 * i), rows_at(192 + 16 * i))
        return carry

    lax.fori_loop(0, 4, field_rows, 0)
    loads[2].wait()

    def mix_tile(k, carry):
        spec = jnp.dot(f_v[k], yb[k], preferred_element_type=F32)
        sr, si = spec[:128], spec[128:]
        fr, fi = fs[k, :128, :], fs[k, 128:, :]
        tr, ti = flip(sr), flip(si)
        special = jnp.logical_and(row0, k == 0)
        mixed_re = jnp.where(special, fr * sr, fr * sr - fi * si)
        mixed_im = jnp.where(special, fi * si, fr * si + fi * sr)
        grad_re = jnp.where(special, tr * sr, tr * sr + ti * si)
        grad_im = jnp.where(special, ti * si, ti * sr - tr * si)
        mixed = jnp.concatenate(
            [
                jnp.concatenate([mixed_re, grad_re], axis=1),
                jnp.concatenate([mixed_im, grad_im], axis=1),
            ],
            axis=0,
        ).astype(BF16)
        zb[k] = jnp.dot(g_v[k], mixed, preferred_element_type=F32)
        return carry

    lax.fori_loop(0, 16, mix_tile, 0, unroll=16)
    round_x_third()


    def back_rows(i, carry):
        lo, hi = rows_at(16 * i), rows_at(128 + 16 * i)
        spectra = [(zb[0, lo, :128], None)]
        spectra += [(zb[k, lo, :128], zb[k, hi, :128]) for k in range(1, 16)]
        spectra += [(zb[0, hi, :128], None)]
        for a, restored in enumerate(real_inverse(32, spectra, half=True)):
            turned = flip(restored)
            out = rows_at(128 * a + 16 * i)
            gp[out, :128] = (turned * bv[a, lo, :].astype(F32)).astype(BF16)
            gp[out, 128:] = (turned * qvb[a % 8, a // 8, lo, :].astype(F32)).astype(BF16)
        return carry

    lax.fori_loop(0, 8, back_rows, 0)


    for piece in range(4):
        for k in range(CHUNKS):
            t_sibling(piece, k, oc).wait_recv()

    def weight_rows(h, core):
        lhs = tb[h, core].reshape(2048, 128)
        return lax.dot_general(lhs, gp[...], (((0,), (0,)), ((), ())), preferred_element_type=F32)

    away_parts = [weight_rows(ox, core) for core in range(2)]
    for core in range(2):
        rsend[core * 128 : core * 128 + 128, :] = away_parts[core][:, :128].astype(BF16)
    rsend[256:, :] = jnp.where(low128, away_parts[0][:, 128:], flip(away_parts[1][:, 128:])).astype(BF16)
    weight_out = remote(rsend, rrecv, pair_s.at[3], pair_r.at[3], l_partner)
    weight_out.start()

    loads[3].wait()

    def filter_grad_step(k, carry):
        sums = []
        for l in range(2):
            block = z + 8 * l
            total = carry[l] + ct_v[block, pl.ds(k, 1), :] * zb[k, :128, 128:]
            sums.append(total + ct_v[block, pl.ds(k + 16, 1), :] * zb[k, 128:, 128:])
        return tuple(sums)

    zero = jnp.zeros((128, 128), F32)
    near, far = lax.fori_loop(0, 16, filter_grad_step, (zero, zero))
    own = jnp.where(first, near, far)
    other = jnp.where(first, far, near)
    fsend[...] = jnp.where(low64, other[:64], flip(other[64:]))
    filter_out = remote(fsend, frecv, pair_s.at[4], pair_r.at[4], l_partner)
    filter_out.start()
    fown[...] = own

    for core in range(2):
        rown[core * 128 : core * 128 + 128, :] = weight_rows(xl, core)

    def unfolded(mine, got):
        turned, turned_mine = flip(got), flip(mine)
        low = lax.broadcasted_iota(jnp.int32, mine.shape, 1) < 64
        as_first = jnp.where(low, mine, jnp.concatenate([turned, got], axis=0))
        as_second = jnp.where(low, jnp.concatenate([got, turned], axis=0), turned_mine)
        return jnp.where(first, as_first, as_second)

    weight_out.wait_recv()
    mine = rown[:, :128]
    got = rrecv[:256, :].astype(F32)
    mine_turned, got_turned = flip(mine), flip(got)
    low256 = lax.broadcasted_iota(jnp.int32, (256, 128), 1) < 64
    wg_ref[0] = jnp.where(
        first, jnp.where(low256, mine_turned, got), jnp.where(low256, got_turned, mine)
    )
    wg_ref[1] = jnp.where(
        first, jnp.where(low256, mine, got_turned), jnp.where(low256, got, mine_turned)
    )
    wg_ref[2] = unfolded(rown[:, 128:], rrecv[256:, :].astype(F32))
    filter_out.wait_recv()
    fg_ref[...] = unfolded(fown[...], frecv[...])

    for spread in (tok_a, tok_b, gate_a, gate_b, proj_a, proj_b):
        spread.drain()
    for sent in (tok_pair_out, gate_out, proj_out, weight_out, filter_out):
        sent.wait_send()
    for side in range(2):
        for away, index in index_of.items():
            sib_copy(side, index, away, c).wait_send()

    for away in index_of:

        @pl.when(turn(y, away) != z)
        def _():
            turn_copy(away).wait_send()

    for k in range(CHUNKS):
        for way in range(2):
            along_x(way, k).wait_send()
            half_on(way, k).wait_send()
        for piece in range(4):
            t_sibling(piece, k, c).wait_send()


def on_device(tables, tokens, in_weight, filter_taps, grad_out):
    forward, inverse, single = tables
    vmem = pl.BlockSpec(memory_space=pltpu.VMEM)
    anywhere = pl.BlockSpec(memory_space=pltpu.HBM)
    dma = pltpu.SemaphoreType.DMA
    ring_sems = [dma((8,)) for _ in range(12)]
    weight_grad, filter_grad = pl.pallas_call(
        kernel,
        out_shape=(
            jax.ShapeDtypeStruct((3, 256, 128), F32),
            jax.ShapeDtypeStruct((128, 128), F32),
        ),
        in_specs=[anywhere] * 7,
        out_specs=(vmem, vmem),
        scratch_shapes=[
            pltpu.VMEM((128, 128), BF16),
            pltpu.VMEM((128, 128), F32),
            pltpu.VMEM((3, 4096, 128), BF16),
            pltpu.VMEM((16, 256, 256), BF16),
            pltpu.VMEM((16, 256, 256), BF16),
            pltpu.VMEM((16, 32, 128), F32),
            pltpu.VMEM((2, 8, 2, 128, 128), BF16),
            pltpu.VMEM((8, 2, 128, 128), BF16),
            pltpu.VMEM((128, 128), BF16),
            pltpu.VMEM((8, 2, 192, 128), BF16),
            pltpu.VMEM((192, 128), BF16),
            pltpu.VMEM((2, 2, 2, 8, 128, 128), BF16),
            pltpu.VMEM((128, 384), F32),
            pltpu.VMEM((16, 128, 128), BF16),
            pltpu.VMEM((16, 256, 128), BF16),
            pltpu.VMEM((16, 256, 128), F32),
            pltpu.VMEM((16, 256, 256), F32),
            pltpu.VMEM((2048, 256), BF16),
            pltpu.VMEM((256, 256), F32),
            pltpu.VMEM((384, 128), BF16),
            pltpu.VMEM((384, 128), BF16),
            pltpu.VMEM((128, 128), F32),
            pltpu.VMEM((64, 128), F32),
            pltpu.VMEM((64, 128), F32),
            dma((7,)),
            *ring_sems,
            dma((5,)), dma((5,)),
            dma((2, 8)), dma((2, 8)),
            dma((8,)), dma((8,)),
            dma((2, CHUNKS)), dma((2, CHUNKS)),
            dma((2, CHUNKS)), dma((2, CHUNKS)),
            dma((4, CHUNKS)), dma((4, CHUNKS)),
        ],
        compiler_params=pltpu.CompilerParams(
            collective_id=0, has_side_effects=True, vmem_limit_bytes=52 * 1024 * 1024
        ),
        cost_estimate=pl.CostEstimate(flops=3_000_000_000, bytes_accessed=10_000_000, transcendentals=0),
    )(
        tokens,
        grad_out,
        filter_taps,
        jnp.transpose(in_weight, (1, 0, 2)),
        forward,
        inverse,
        single,
    )
    return jnp.transpose(weight_grad, (1, 0, 2)), filter_grad


def solution(mesh):
    tables = transform_tables()

    def whole(tokens, in_weight, filter_taps, grad_out):
        constants = tuple(jnp.asarray(t) for t in tables)
        placed = (P("ctx", "ch"), P(None, None, "ch"), P("ctx", "ch"), P("ctx", "ch"))
        return jax.shard_map(
            on_device,
            mesh=mesh,
            in_specs=((P(), P(), P()),) + placed,
            out_specs=(P("ctx", None, "ch"), P("ctx", "ch")),
            check_vma=False,
        )(constants, tokens, in_weight, filter_taps, grad_out)

    return whole
```

```python
import math

import jax
import jax.numpy as jnp
import ml_dtypes
import numpy as np
from jax import lax
from jax.experimental import pallas as pl
from jax.experimental.pallas import tpu as pltpu
from jax.sharding import PartitionSpec as P

MESH = pl.DeviceIdType.MESH
BF16 = jnp.bfloat16
F32 = jnp.float32
ROWS = 128
TILES = 16
CHUNKS = 2
PER = 8 // CHUNKS


def transform_tables():
    r = np.arange(128)
    k1 = np.arange(128)
    forward = np.zeros((16, 256, 256))
    inverse = np.zeros((16, 256, 256))
    for k2 in range(1, 16):
        angle = 2 * np.pi * (((k2 + 32 * k1)[:, None] * r[None, :]) % 4096) / 4096
        c, s = np.cos(angle), np.sin(angle)
        forward[k2] = np.block([[c, s], [-s, c]])
        inverse[k2] = np.block([[c.T, -s.T], [s.T, c.T]]) * (2 / 4096)
    k1 = np.arange(64)
    a0 = 2 * np.pi * ((32 * k1[:, None] * r[None, :]) % 4096) / 4096
    a16 = 2 * np.pi * (((16 + 32 * k1)[:, None] * r[None, :]) % 4096) / 4096
    nyquist = 1.0 - 2.0 * (r % 2)
    re0, im0 = np.cos(a0), -np.sin(a0)
    im0[0] = nyquist
    zero = np.zeros((64, 128))
    forward[0] = np.block(
        [
            [re0, zero],
            [zero, np.cos(a16)],
            [im0, zero],
            [zero, -np.sin(a16)],
        ]
    )
    back_re0, back_im0 = 2 * np.cos(a0).T, -2 * np.sin(a0).T
    back_re0[:, 0] = 1.0
    back_im0[:, 0] = nyquist
    zero = np.zeros((128, 64))
    inverse[0] = (
        np.block(
            [
                [back_re0, zero, back_im0, zero],
                [zero, 2 * np.cos(a16).T, zero, -2 * np.sin(a16).T],
            ]
        )
        / 4096
    )
    block = np.arange(16)[:, None]
    k = np.arange(16)[None, :]
    angle = 2 * np.pi * ((block * k) % 32) / 32
    im_part = -np.sin(angle)
    im_part[:, 0] = 1.0 - 2.0 * (np.arange(16) % 2)
    single = np.concatenate([np.cos(angle), im_part], axis=1)
    single = np.broadcast_to(single[:, :, None], (16, 32, 128))
    return (
        forward.astype(ml_dtypes.bfloat16),
        inverse.astype(ml_dtypes.bfloat16),
        single.astype(np.float32),
    )


def root(n, a, sign):
    angle = -sign * 2 * math.pi * a / n
    return math.cos(angle), math.sin(angle)


def times(v, w):
    re, im = v
    wr, wi = w
    if abs(wi) < 1e-12:
        return (re, im) if wr > 0 else (-re, -im)
    if abs(wr) < 1e-12:
        return (-im, re) if wi > 0 else (im, -re)
    return re * wr - im * wi, re * wi + im * wr


def complex_dft(u, sign):
    n = len(u)
    if n == 1:
        return u
    h = n // 2
    low = [(u[a][0] + u[a + h][0], u[a][1] + u[a + h][1]) for a in range(h)]
    high = [
        times((u[a][0] - u[a + h][0], u[a][1] - u[a + h][1]), root(n, a, sign))
        for a in range(h)
    ]
    even, odd = complex_dft(low, sign), complex_dft(high, sign)
    return [even[i // 2] if i % 2 == 0 else odd[i // 2] for i in range(n)]


def real_forward(n, x):
    if n == 2:
        return [(x[0] + x[1], None), (x[0] - x[1], None)]
    h, q = n // 2, n // 4
    if len(x) == h:
        fold, diff = x, x
    else:
        fold = [x[a] + x[a + h] for a in range(h)]
        diff = [x[a] - x[a + h] for a in range(h)]
    even = real_forward(h, fold)
    odd = complex_dft(
        [times((diff[a], -diff[a + q]), root(n, a, 1)) for a in range(q)], 1
    )
    out = [None] * (h + 1)
    for m in range(h // 2 + 1):
        out[2 * m] = even[m]
    for j in range(q):
        k = 4 * j + 1
        if k <= h:
            out[k] = odd[j]
        else:
            out[n - k] = (odd[j][0], -odd[j][1])
    return out


def real_inverse(n, z, half=False):
    if n == 2:
        return [z[0][0] + z[1][0], z[0][0] - z[1][0]]
    h, q = n // 2, n // 4
    even = real_inverse(h, z[0::2])
    v = []
    for j in range(q):
        k = 4 * j + 1
        v.append(z[k] if k <= h else (z[n - k][0], -z[n - k][1]))
    s = complex_dft(v, -1)
    t = [times(s[a], root(n, a, -1)) for a in range(q)]
    odd = [t[a][0] for a in range(q)] + [-t[a][1] for a in range(q)]
    low = [even[a] + odd[a] for a in range(h)]
    return low if half else low + [even[a] - odd[a] for a in range(h)]


class Spread:
    def __init__(self, slot, rows, place, to, send_sem, recv_sem):
        self.slot, self.rows, self.place, self.to = slot, rows, place, to
        self.send_sem, self.recv_sem = send_sem, recv_sem
        self.sent = 0

    def piece(self, origin):
        return self.slot(lax.rem(self.place + 8 + origin, 8))

    def copy(self, ref, seen, device):
        at = {-2: 0, 2: 1, -1: 2, 1: 2}.get(seen, 3)
        return pltpu.make_async_remote_copy(
            src_ref=ref, dst_ref=ref, send_sem=self.send_sem, recv_sem=self.recv_sem.at[at],
            device_id=device, device_id_type=MESH,
        )

    def send(self, origin, distance, half=None):
        ref, rows = self.piece(origin), self.rows
        if half is not None:
            rows = rows // 2
            ref = ref.at[pl.ds(half * rows, rows)]
        self.copy(ref, origin - distance, self.to(distance)).start()
        self.sent += rows

    def wait(self, pieces, seen, total):
        self.copy(total.at[pl.ds(0, pieces * self.rows)], seen, self.to(1)).wait_recv()

    def first(self):
        for distance in (2, -2, 1, -1):
            self.send(0, distance)

    def middle(self, total):
        self.wait(1, -2, total)
        self.send(-2, 2, 0)
        self.send(-2, 1)
        self.wait(1, 2, total)
        self.send(2, -2, 1)
        self.send(2, -1)
        self.wait(2, 1, total)

    def last(self, total):
        self.wait(3, 3, total)

    def drain(self, total):
        self.copy(total.at[pl.ds(0, self.sent)], 1, self.to(1)).wait_send()


def kernel(
    tok_hbm, go_hbm, taps_hbm, w_hbm, f_hbm, g_hbm, ct_hbm,
    wg_ref, fg_ref,
    go_v, taps_v, w_v, f_v, g_v, ct_v, tokb, gtb, gtx, qvb, qvx, tb, acc, bv, yb, fs, zb, gp,
    rown, rsend, rrecv, fown, fsend, frecv,
    local_sem, spread_s, tok_a_r, tok_b_r, gate_a_r, gate_b_r, proj_a_r, proj_b_r,
    pair_s, pair_r, sib_s, sib_r, tr_s, tr_r, tx_s, tx_r, tx2_r, ts_s, ts_r,
):
    ctx, ch = lax.axis_index("ctx"), lax.axis_index("ch")
    xl, z = ctx // 8, lax.rem(ctx, 8)
    c, xh, y = lax.rem(ch, 2), ch // 16, lax.rem(ch // 2, 8)
    ox, oh, oc = 1 - xl, 1 - xh, 1 - c

    def dev(xh_, xl_, y_, z_, c_):
        return (xl_ * 8 + z_, (xh_ * 8 + y_) * 2 + c_)

    def remote(src, dst, s, r, to):
        return pltpu.make_async_remote_copy(
            src_ref=src, dst_ref=dst, send_sem=s, recv_sem=r, device_id=to, device_id_type=MESH
        )

    def turn(v, by):
        return lax.rem(v + 8 + by, 8)

    def along(axis):
        if axis == "y":
            return lambda by: dev(xh, xl, turn(y, by), z, c)
        return lambda by: dev(xh, xl, y, turn(z, by), c)

    sibling = dev(xh, xl, y, z, oc)
    h_partner = dev(oh, xl, y, z, c)
    l_partner = dev(xh, ox, y, z, c)
    place = 2 * xh + xl
    x_up, x_down = lax.rem(place + 1, 4), lax.rem(place + 3, 4)
    x_right = dev(x_up // 2, lax.rem(x_up, 2), y, z, c)
    x_left = dev(x_down // 2, lax.rem(x_down, 2), y, z, c)

    barrier = pltpu.get_barrier_semaphore()
    peers = [sibling] + [along("y")(by) for by in (-2, -1, 1, 2)]
    peers += [along("z")(by) for by in range(1, 8)]
    for by in range(1, 4):
        other = lax.rem(place + by, 4)
        peers.append(dev(other // 2, lax.rem(other, 2), y, z, c))
    for peer in peers:
        pl.semaphore_signal(barrier, inc=1, device_id=peer, device_id_type=MESH)

    own_loads = [
        pltpu.make_async_copy(go_hbm, go_v, local_sem.at[4]),
        pltpu.make_async_copy(taps_hbm, taps_v, local_sem.at[5]),
        pltpu.make_async_copy(tok_hbm, tokb.at[xh, y, c], local_sem.at[6]),
    ]
    for load in own_loads:
        load.start()
    loads = [
        pltpu.make_async_copy(w_hbm, w_v, local_sem.at[0]),
        pltpu.make_async_copy(f_hbm, f_v, local_sem.at[1]),
        pltpu.make_async_copy(g_hbm, g_v, local_sem.at[2]),
        pltpu.make_async_copy(ct_hbm, ct_v, local_sem.at[3]),
    ]
    for load in loads:
        load.start()

    lane = lax.broadcasted_iota(jnp.int32, (64, 128), 1)
    low64 = lane < 64
    low128 = lax.broadcasted_iota(jnp.int32, (128, 128), 1) < 64

    def flip(v):
        return pltpu.roll(v, 64, 1)

    def fold_low(v, h):
        top, bottom = v[:64], v[64:]
        return jnp.where(low64, top, flip(bottom)) if h == 0 else jnp.where(low64, flip(top), bottom)

    def fold_high(v, h):
        top, bottom = v[:64], v[64:]
        return jnp.where(low64, bottom, flip(top)) if h == 0 else jnp.where(low64, flip(bottom), top)

    for load in own_loads:
        load.wait()
    go = go_v[...].astype(F32)
    taps = taps_v[...]
    packs = [
        jnp.concatenate([fold_high(go, h), fold_low(taps, h)], axis=0).astype(BF16)
        for h in range(2)
    ]
    first = xl == 0
    gtb[z, xl] = jnp.where(first, packs[0], packs[1])
    gtx[...] = jnp.where(first, packs[1], packs[0])

    pl.semaphore_wait(barrier, len(peers))

    tok_a = Spread(lambda q: tokb.at[xh, q, c], 128, y, along("y"), spread_s.at[0], tok_a_r)
    tok_b = Spread(lambda q: tokb.at[oh, q, c], 128, y, along("y"), spread_s.at[1], tok_b_r)
    gate_a = Spread(lambda q: gtb.at[q, xl], 128, z, along("z"), spread_s.at[2], gate_a_r)
    gate_b = Spread(lambda q: gtb.at[q, ox], 128, z, along("z"), spread_s.at[3], gate_b_r)
    proj_a = Spread(lambda q: qvb.at[q, xl], 192, z, along("z"), spread_s.at[4], proj_a_r)
    proj_b = Spread(lambda q: qvb.at[q, ox], 192, z, along("z"), spread_s.at[5], proj_b_r)

    total = w_v.at[0]
    index_of = {0: 0, -1: 1, -2: 2, -3: 3, -4: 4, 3: 5, 2: 6, 1: 7}

    def sib_copy(ref, group):
        return remote(ref, ref, sib_s.at[0], sib_r.at[group], sibling)

    def to_sibling(side, aways, group):
        for away in aways:
            sib_copy(tokb.at[xh if side == 0 else oh, turn(y, away), c], group).start()

    def from_sibling(pieces, group):
        sib_copy(total.at[pl.ds(0, 128 * pieces)], group).wait_recv()

    tok_pair_out = remote(tokb.at[xh, y, c], tokb.at[xh, y, c], pair_s.at[0], pair_r.at[0], h_partner)
    tok_pair_in = remote(tokb.at[oh, y, c], tokb.at[oh, y, c], pair_s.at[0], pair_r.at[0], h_partner)
    gate_out = remote(gtx, gtb.at[z, xl], pair_s.at[1], pair_r.at[1], l_partner)
    gate_in = remote(gtx, gtb.at[z, ox], pair_s.at[1], pair_r.at[1], l_partner)
    proj_out = remote(qvx, qvb.at[z, xl], pair_s.at[2], pair_r.at[2], l_partner)
    proj_in = remote(qvx, qvb.at[z, ox], pair_s.at[2], pair_r.at[2], l_partner)

    def turn_copy(away):
        q = turn(y, away)
        return remote(
            tokb.at[xh, q, c], tb.at[xh, c, xl, z], tr_s.at[0], tr_r.at[0], dev(xh, xl, y, q, c)
        )

    def turned_over(aways):
        for away in aways:
            q = turn(y, away)

            @pl.when(q == z)
            def _():
                tb[xh, c, xl, z] = tokb[xh, q, c]

            @pl.when(q != z)
            def _():
                turn_copy(away).start()

    def project(aways):
        summed = None
        for away in aways:
            for side in range(2):
                q = turn(y, away)
                h = xh if side == 0 else oh
                left = jnp.concatenate([tokb[h, q, 0], tokb[h, q, 1]], axis=1)
                rows = pl.ds(pl.multiple_of((h * 8 + q) * 256, 256), 256)
                right = jnp.concatenate([w_v[j, rows, :] for j in range(3)], axis=1)
                term = jnp.dot(left, right, preferred_element_type=F32)
                summed = term if summed is None else summed + term
        return summed

    tok_pair_out.start()
    tok_a.first()
    to_sibling(0, [0], 0)
    gate_out.start()
    gate_a.first()
    turned_over([0])
    tok_pair_in.wait_recv()
    tok_b.first()
    to_sibling(1, [0], 0)
    gate_in.wait_recv()
    gate_b.first()
    loads[0].wait()
    near, far = [-2, 2, -1, 1], [-3, 3, -4]
    tok_a.middle(total)
    to_sibling(0, near, 1)
    turned_over(near)
    from_sibling(2, 0)
    acc[...] = project([0])
    tok_b.middle(total)
    to_sibling(1, near, 1)
    gate_a.middle(total)
    gate_b.middle(total)
    tok_a.last(total)
    to_sibling(0, far, 2)
    turned_over(far)
    from_sibling(8, 1)
    acc[...] += project(near)
    tok_b.last(total)
    to_sibling(1, far, 2)
    from_sibling(6, 2)
    projected = (acc[...] + project(far)).astype(BF16).astype(F32)

    qp, kp, vp = projected[:, :128], projected[:, 128:256], projected[:, 256:]
    both = []
    for h in range(2):
        kq = jnp.where(low128, kp, flip(qp)) if h == 0 else jnp.where(low128, flip(kp), qp)
        both.append(jnp.concatenate([kq, fold_low(vp, h)], axis=0).astype(BF16))
    qvx[...] = jnp.where(first, both[1], both[0])
    proj_out.start()
    qvb[z, xl] = jnp.where(first, both[0], both[1])
    proj_a.first()


    up_h, up_l = x_up // 2, lax.rem(x_up, 2)
    down_h, down_l = x_down // 2, lax.rem(x_down, 2)

    def block_of(h, core, l, k):
        return tb.at[h, core, l, pl.ds(PER * k, PER)]

    def along_x(way, k):
        ref = block_of(xh, c, xl, k)
        return remote(ref, ref, tx_s.at[0], tx_r.at[way, k], x_right if way == 0 else x_left)

    def from_x(way, k):
        ref = block_of(down_h, c, down_l, k) if way == 0 else block_of(up_h, c, up_l, k)
        return remote(ref, ref, tx_s.at[0], tx_r.at[way, k], x_right if way == 0 else x_left)

    def half_on(way, k):
        h, l = (down_h, down_l) if way == 0 else (up_h, up_l)
        ref = tb.at[h, c, l, pl.ds(PER * k + PER // 2 * way, PER // 2)]
        return remote(ref, ref, tx_s.at[0], tx2_r.at[k], x_right if way == 0 else x_left)

    def across(k):
        ref = block_of(oh, c, xl, k)
        return remote(ref, ref, tx_s.at[0], tx2_r.at[k], x_right)

    piece_at = [(xh, xl), (down_h, down_l), (up_h, up_l), (oh, xl)]

    def t_sibling(piece, k, core):
        h, l = piece_at[piece]
        ref = block_of(h, core, l, k)
        return remote(ref, ref, ts_s.at[0], ts_r.at[0], sibling)

    def count(s, r, rows):
        ref = total.at[pl.ds(0, rows)]
        return remote(ref, ref, s, r, sibling)

    def round_x_first():
        count(tr_s.at[0], tr_r.at[0], 7 * 128).wait_recv()
        for k in range(CHUNKS):
            along_x(0, k).start()
            along_x(1, k).start()
            t_sibling(0, k, c).start()

    def round_x_second():
        for k in range(CHUNKS):
            from_x(0, k).wait_recv()
            half_on(0, k).start()
            from_x(1, k).wait_recv()
            half_on(1, k).start()
            t_sibling(1, k, c).start()
            t_sibling(2, k, c).start()

    def round_x_third():
        for k in range(CHUNKS):
            across(k).wait_recv()
            t_sibling(3, k, c).start()

    round_x_first()
    proj_in.wait_recv()
    proj_b.first()
    gate_a.last(total)
    gate_b.last(total)


    def put_spectra(x, rows_lo, rows_hi):
        spectra = real_forward(32, x)
        yb[0, rows_lo, :] = spectra[0][0].astype(BF16)
        yb[0, rows_hi, :] = spectra[16][0].astype(BF16)
        for k in range(1, 16):
            yb[k, rows_lo, :] = spectra[k][0].astype(BF16)
            yb[k, rows_hi, :] = spectra[k][1].astype(BF16)

    low16 = lax.broadcasted_iota(jnp.int32, (16, 128), 1) < 64

    def rows_at(start):
        return pl.ds(pl.multiple_of(start, 16), 16)

    def filter_rows(i, carry):
        top, bottom = [], []
        for a in range(16):
            packed = gtb[a % 8, a // 8, rows_at(64 + 16 * i), :].astype(F32)
            turned = flip(packed)
            top.append(jnp.where(low16, packed, turned))
            bottom.append(jnp.where(low16, turned, packed))
        put_spectra(top, rows_at(16 * i), rows_at(128 + 16 * i))
        put_spectra(bottom, rows_at(64 + 16 * i), rows_at(192 + 16 * i))
        return carry

    lax.fori_loop(0, 4, filter_rows, 0)
    loads[1].wait()
    row0 = lax.broadcasted_iota(jnp.int32, (128, 128), 0) == 0

    def filter_tile(k, carry):
        spec = jnp.dot(f_v[k], yb[k], preferred_element_type=F32)
        fs[k, :128, :] = spec[:128]
        im = spec[128:]
        special = jnp.logical_and(row0, k == 0)
        fs[k, 128:, :] = jnp.where(jnp.logical_or(low128, special), im, -im)
        return carry

    lax.fori_loop(0, 16, filter_tile, 0, unroll=16)

    proj_a.middle(total)
    proj_b.middle(total)
    round_x_second()
    proj_a.last(total)
    proj_b.last(total)


    def field_rows(i, carry):
        top, bottom = [], []
        for a in range(16):
            za, la = a % 8, a // 8
            vals = qvb[za, la, rows_at(128 + 16 * i), :].astype(F32)
            gos = gtb[za, la, rows_at(16 * i), :].astype(F32)
            b_top = jnp.where(low16, vals, gos)
            b_bottom = flip(jnp.where(low16, gos, vals))
            bv[a, rows_at(16 * i), :] = b_top.astype(BF16)
            bv[a, rows_at(64 + 16 * i), :] = b_bottom.astype(BF16)
            top.append(qvb[za, la, rows_at(16 * i), :].astype(F32) * b_top)
            bottom.append(qvb[za, la, rows_at(64 + 16 * i), :].astype(F32) * b_bottom)
        put_spectra(top, rows_at(16 * i), rows_at(128 + 16 * i))
        put_spectra(bottom, rows_at(64 + 16 * i), rows_at(192 + 16 * i))
        return carry

    lax.fori_loop(0, 4, field_rows, 0, unroll=4)
    round_x_third()
    loads[2].wait()

    def mix_tile(k, carry):
        spec = jnp.dot(f_v[k], yb[k], preferred_element_type=F32)
        sr, si = spec[:128], spec[128:]
        fr, fi = fs[k, :128, :], fs[k, 128:, :]
        tr, ti = flip(sr), flip(si)
        special = jnp.logical_and(row0, k == 0)
        mixed_re = jnp.where(special, fr * sr, fr * sr - fi * si)
        mixed_im = jnp.where(special, fi * si, fr * si + fi * sr)
        grad_re = jnp.where(special, tr * sr, tr * sr + ti * si)
        grad_im = jnp.where(special, ti * si, ti * sr - tr * si)
        mixed = jnp.concatenate([mixed_re, mixed_im], axis=0).astype(BF16)
        zb[k] = jnp.dot(g_v[k], mixed, preferred_element_type=F32)
        yb[k] = jnp.concatenate([grad_re, grad_im], axis=0).astype(BF16)
        return carry

    lax.fori_loop(0, 16, mix_tile, 0, unroll=16)


    def back_rows(i, carry):
        lo, hi = rows_at(16 * i), rows_at(128 + 16 * i)
        spectra = [(zb[0, lo, :], None)]
        spectra += [(zb[k, lo, :], zb[k, hi, :]) for k in range(1, 16)]
        spectra += [(zb[0, hi, :], None)]
        for a, restored in enumerate(real_inverse(32, spectra, half=True)):
            turned = flip(restored)
            out = rows_at(128 * a + 16 * i)
            gp[out, :128] = (turned * bv[a, lo, :].astype(F32)).astype(BF16)
            gp[out, 128:] = (turned * qvb[a % 8, a // 8, lo, :].astype(F32)).astype(BF16)
        return carry

    lax.fori_loop(0, 8, back_rows, 0, unroll=2)


    count(ts_s.at[0], ts_r.at[0], 4096).wait_recv()

    def weight_rows(h, core):
        lhs = tb[h, core].reshape(2048, 128)
        return lax.dot_general(lhs, gp[...], (((0,), (0,)), ((), ())), preferred_element_type=F32)

    away_parts = [weight_rows(ox, core) for core in range(2)]
    for core in range(2):
        rsend[core * 128 : core * 128 + 128, :] = away_parts[core][:, :128].astype(BF16)
    rsend[256:, :] = jnp.where(low128, away_parts[0][:, 128:], flip(away_parts[1][:, 128:])).astype(BF16)
    weight_out = remote(rsend, rrecv, pair_s.at[3], pair_r.at[3], l_partner)
    weight_out.start()

    loads[3].wait()

    def filter_grad_step(k, carry):
        sums = []
        back = jnp.dot(g_v[k], yb[k], preferred_element_type=F32)
        for l in range(2):
            block = z + 8 * l
            total = carry[l] + ct_v[block, pl.ds(k, 1), :] * back[:128]
            sums.append(total + ct_v[block, pl.ds(k + 16, 1), :] * back[128:])
        return tuple(sums)

    zero = jnp.zeros((128, 128), F32)
    near, far = lax.fori_loop(0, 16, filter_grad_step, (zero, zero), unroll=16)
    own = jnp.where(first, near, far)
    other = jnp.where(first, far, near)
    fsend[...] = jnp.where(low64, other[:64], flip(other[64:]))
    filter_out = remote(fsend, frecv, pair_s.at[4], pair_r.at[4], l_partner)
    filter_out.start()
    fown[...] = own

    for core in range(2):
        rown[core * 128 : core * 128 + 128, :] = weight_rows(xl, core)

    def unfolded(mine, got):
        turned, turned_mine = flip(got), flip(mine)
        low = lax.broadcasted_iota(jnp.int32, mine.shape, 1) < 64
        as_first = jnp.where(low, mine, jnp.concatenate([turned, got], axis=0))
        as_second = jnp.where(low, jnp.concatenate([got, turned], axis=0), turned_mine)
        return jnp.where(first, as_first, as_second)

    weight_out.wait_recv()
    mine = rown[:, :128]
    got = rrecv[:256, :].astype(F32)
    mine_turned, got_turned = flip(mine), flip(got)
    low256 = lax.broadcasted_iota(jnp.int32, (256, 128), 1) < 64
    wg_ref[0] = jnp.where(
        first, jnp.where(low256, mine_turned, got), jnp.where(low256, got_turned, mine)
    )
    wg_ref[1] = jnp.where(
        first, jnp.where(low256, mine, got_turned), jnp.where(low256, got, mine_turned)
    )
    wg_ref[2] = unfolded(rown[:, 128:], rrecv[256:, :].astype(F32))
    filter_out.wait_recv()
    fg_ref[...] = unfolded(fown[...], frecv[...])

    for spread in (tok_a, tok_b, gate_a, gate_b, proj_a, proj_b):
        spread.drain(total)
    for sent in (tok_pair_out, gate_out, proj_out, weight_out, filter_out):
        sent.wait_send()
    for s, rows in ((sib_s, 16 * 128), (tr_s, 7 * 128), (tx_s, 3072), (ts_s, 4096)):
        count(s.at[0], sib_r.at[0], rows).wait_send()


def on_device(tables, tokens, in_weight, filter_taps, grad_out):
    forward, inverse, single = tables
    vmem = pl.BlockSpec(memory_space=pltpu.VMEM)
    anywhere = pl.BlockSpec(memory_space=pltpu.HBM)
    dma = pltpu.SemaphoreType.DMA
    weight_grad, filter_grad = pl.pallas_call(
        kernel,
        out_shape=(
            jax.ShapeDtypeStruct((3, 256, 128), F32),
            jax.ShapeDtypeStruct((128, 128), F32),
        ),
        in_specs=[anywhere] * 7,
        out_specs=(vmem, vmem),
        scratch_shapes=[
            pltpu.VMEM((128, 128), BF16),
            pltpu.VMEM((128, 128), F32),
            pltpu.VMEM((3, 4096, 128), BF16),
            pltpu.VMEM((16, 256, 256), BF16),
            pltpu.VMEM((16, 256, 256), BF16),
            pltpu.VMEM((16, 32, 128), F32),
            pltpu.VMEM((2, 8, 2, 128, 128), BF16),
            pltpu.VMEM((8, 2, 128, 128), BF16),
            pltpu.VMEM((128, 128), BF16),
            pltpu.VMEM((8, 2, 192, 128), BF16),
            pltpu.VMEM((192, 128), BF16),
            pltpu.VMEM((2, 2, 2, 8, 128, 128), BF16),
            pltpu.VMEM((128, 384), F32),
            pltpu.VMEM((16, 128, 128), BF16),
            pltpu.VMEM((16, 256, 128), BF16),
            pltpu.VMEM((16, 256, 128), F32),
            pltpu.VMEM((16, 256, 128), F32),
            pltpu.VMEM((2048, 256), BF16),
            pltpu.VMEM((256, 256), F32),
            pltpu.VMEM((384, 128), BF16),
            pltpu.VMEM((384, 128), BF16),
            pltpu.VMEM((128, 128), F32),
            pltpu.VMEM((64, 128), F32),
            pltpu.VMEM((64, 128), F32),
            dma((7,)),
            dma((6,)),
            *[dma((4,)) for _ in range(6)],
            dma((5,)), dma((5,)),
            dma((1,)), dma((3,)),
            dma((1,)), dma((1,)),
            dma((1,)), dma((2, CHUNKS)), dma((CHUNKS,)),
            dma((1,)), dma((1,)),
        ],
        compiler_params=pltpu.CompilerParams(
            collective_id=0, has_side_effects=True, vmem_limit_bytes=63 * 1024 * 1024
        ),
        cost_estimate=pl.CostEstimate(flops=3_000_000_000, bytes_accessed=10_000_000, transcendentals=0),
    )(
        tokens,
        grad_out,
        filter_taps,
        jnp.transpose(in_weight, (1, 0, 2)),
        forward,
        inverse,
        single,
    )
    return jnp.transpose(weight_grad, (1, 0, 2)), filter_grad


def solution(mesh):
    tables = transform_tables()

    def whole(tokens, in_weight, filter_taps, grad_out):
        constants = tuple(jnp.asarray(t) for t in tables)
        placed = (P("ctx", "ch"), P(None, None, "ch"), P("ctx", "ch"), P("ctx", "ch"))
        return jax.shard_map(
            on_device,
            mesh=mesh,
            in_specs=((P(), P(), P()),) + placed,
            out_specs=(P("ctx", None, "ch"), P("ctx", "ch")),
            check_vma=False,
        )(constants, tokens, in_weight, filter_taps, grad_out)

    return whole
```

```python
import math

import jax
import jax.numpy as jnp
import ml_dtypes
import numpy as np
from jax import lax
from jax.experimental import pallas as pl
from jax.experimental.pallas import tpu as pltpu
from jax.sharding import PartitionSpec as P

MESH = pl.DeviceIdType.MESH
BF16 = jnp.bfloat16
F32 = jnp.float32
ROWS = 128
TILES = 16
CHUNKS = 2
PER = 8 // CHUNKS


def transform_tables():
    r = np.arange(128)
    k1 = np.arange(128)
    forward = np.zeros((16, 256, 256))
    inverse = np.zeros((16, 256, 256))
    for k2 in range(1, 16):
        angle = 2 * np.pi * (((k2 + 32 * k1)[:, None] * r[None, :]) % 4096) / 4096
        c, s = np.cos(angle), np.sin(angle)
        forward[k2] = np.block([[c, s], [-s, c]])
        inverse[k2] = np.block([[c.T, -s.T], [s.T, c.T]]) * (2 / 4096)
    k1 = np.arange(64)
    a0 = 2 * np.pi * ((32 * k1[:, None] * r[None, :]) % 4096) / 4096
    a16 = 2 * np.pi * (((16 + 32 * k1)[:, None] * r[None, :]) % 4096) / 4096
    nyquist = 1.0 - 2.0 * (r % 2)
    re0, im0 = np.cos(a0), -np.sin(a0)
    im0[0] = nyquist
    zero = np.zeros((64, 128))
    forward[0] = np.block(
        [
            [re0, zero],
            [zero, np.cos(a16)],
            [im0, zero],
            [zero, -np.sin(a16)],
        ]
    )
    back_re0, back_im0 = 2 * np.cos(a0).T, -2 * np.sin(a0).T
    back_re0[:, 0] = 1.0
    back_im0[:, 0] = nyquist
    zero = np.zeros((128, 64))
    inverse[0] = (
        np.block(
            [
                [back_re0, zero, back_im0, zero],
                [zero, 2 * np.cos(a16).T, zero, -2 * np.sin(a16).T],
            ]
        )
        / 4096
    )
    block = np.arange(16)[:, None]
    k = np.arange(16)[None, :]
    angle = 2 * np.pi * ((block * k) % 32) / 32
    im_part = -np.sin(angle)
    im_part[:, 0] = 1.0 - 2.0 * (np.arange(16) % 2)
    single = np.concatenate([np.cos(angle), im_part], axis=1)
    single = np.broadcast_to(single[:, :, None], (16, 32, 128))
    return (
        forward.astype(ml_dtypes.bfloat16),
        inverse.astype(ml_dtypes.bfloat16),
        single.astype(np.float32),
    )


def root(n, a, sign):
    angle = -sign * 2 * math.pi * a / n
    return math.cos(angle), math.sin(angle)


def times(v, w):
    re, im = v
    wr, wi = w
    if abs(wi) < 1e-12:
        return (re, im) if wr > 0 else (-re, -im)
    if abs(wr) < 1e-12:
        return (-im, re) if wi > 0 else (im, -re)
    return re * wr - im * wi, re * wi + im * wr


def complex_dft(u, sign):
    n = len(u)
    if n == 1:
        return u
    h = n // 2
    low = [(u[a][0] + u[a + h][0], u[a][1] + u[a + h][1]) for a in range(h)]
    high = [
        times((u[a][0] - u[a + h][0], u[a][1] - u[a + h][1]), root(n, a, sign))
        for a in range(h)
    ]
    even, odd = complex_dft(low, sign), complex_dft(high, sign)
    return [even[i // 2] if i % 2 == 0 else odd[i // 2] for i in range(n)]


def real_forward(n, x):
    if n == 2:
        return [(x[0] + x[1], None), (x[0] - x[1], None)]
    h, q = n // 2, n // 4
    if len(x) == h:
        fold, diff = x, x
    else:
        fold = [x[a] + x[a + h] for a in range(h)]
        diff = [x[a] - x[a + h] for a in range(h)]
    even = real_forward(h, fold)
    odd = complex_dft(
        [times((diff[a], -diff[a + q]), root(n, a, 1)) for a in range(q)], 1
    )
    out = [None] * (h + 1)
    for m in range(h // 2 + 1):
        out[2 * m] = even[m]
    for j in range(q):
        k = 4 * j + 1
        if k <= h:
            out[k] = odd[j]
        else:
            out[n - k] = (odd[j][0], -odd[j][1])
    return out


def real_inverse(n, z, half=False):
    if n == 2:
        return [z[0][0] + z[1][0], z[0][0] - z[1][0]]
    h, q = n // 2, n // 4
    even = real_inverse(h, z[0::2])
    v = []
    for j in range(q):
        k = 4 * j + 1
        v.append(z[k] if k <= h else (z[n - k][0], -z[n - k][1]))
    s = complex_dft(v, -1)
    t = [times(s[a], root(n, a, -1)) for a in range(q)]
    odd = [t[a][0] for a in range(q)] + [-t[a][1] for a in range(q)]
    low = [even[a] + odd[a] for a in range(h)]
    return low if half else low + [even[a] - odd[a] for a in range(h)]


class Spread:
    def __init__(self, slot, rows, place, to, send_sem, recv_sem):
        self.slot, self.rows, self.place, self.to = slot, rows, place, to
        self.send_sem, self.recv_sem = send_sem, recv_sem
        self.sent = 0

    def piece(self, origin):
        return self.slot(lax.rem(self.place + 8 + origin, 8))

    def copy(self, ref, seen, device):
        at = {-2: 0, 2: 1, -1: 2, 1: 2}.get(seen, 3)
        return pltpu.make_async_remote_copy(
            src_ref=ref, dst_ref=ref, send_sem=self.send_sem, recv_sem=self.recv_sem.at[at],
            device_id=device, device_id_type=MESH,
        )

    def send(self, origin, distance, half=None):
        ref, rows = self.piece(origin), self.rows
        if half is not None:
            rows = rows // 2
            ref = ref.at[pl.ds(half * rows, rows)]
        self.copy(ref, origin - distance, self.to(distance)).start()
        self.sent += rows

    def wait(self, pieces, seen, total):
        self.copy(total.at[pl.ds(0, pieces * self.rows)], seen, self.to(1)).wait_recv()

    def first(self):
        for distance in (2, -2, 1, -1):
            self.send(0, distance)

    def middle(self, total):
        self.wait(1, -2, total)
        self.send(-2, 2, 0)
        self.send(-2, 1)
        self.wait(1, 2, total)
        self.send(2, -2, 1)
        self.send(2, -1)
        self.wait(2, 1, total)

    def last(self, total):
        self.wait(3, 3, total)

    def drain(self, total):
        self.copy(total.at[pl.ds(0, self.sent)], 1, self.to(1)).wait_send()


def kernel(
    tok_hbm, go_hbm, taps_hbm, w_hbm, f_hbm, g_hbm, ct_hbm,
    wg_ref, fg_ref,
    go_v, taps_v, w_v, f_v, g_v, ct_v, tokb, gtb, gtx, qvb, qvx, tb, acc, bv, yb, fs, zb, gp,
    rown, rsend, rrecv, fown, fsend, frecv,
    local_sem, spread_s, tok_a_r, tok_b_r, gate_a_r, gate_b_r, proj_a_r, proj_b_r,
    pair_s, pair_r, sib_s, sib_r, tr_s, tr_r, tx_s, tx_r, tx2_r, ts_s, ts_r,
):
    ctx, ch = lax.axis_index("ctx"), lax.axis_index("ch")
    xl, z = ctx // 8, lax.rem(ctx, 8)
    c, xh, y = lax.rem(ch, 2), ch // 16, lax.rem(ch // 2, 8)
    ox, oh, oc = 1 - xl, 1 - xh, 1 - c

    def dev(xh_, xl_, y_, z_, c_):
        return (xl_ * 8 + z_, (xh_ * 8 + y_) * 2 + c_)

    def remote(src, dst, s, r, to):
        return pltpu.make_async_remote_copy(
            src_ref=src, dst_ref=dst, send_sem=s, recv_sem=r, device_id=to, device_id_type=MESH
        )

    def turn(v, by):
        return lax.rem(v + 8 + by, 8)

    def along(axis):
        if axis == "y":
            return lambda by: dev(xh, xl, turn(y, by), z, c)
        return lambda by: dev(xh, xl, y, turn(z, by), c)

    sibling = dev(xh, xl, y, z, oc)
    h_partner = dev(oh, xl, y, z, c)
    l_partner = dev(xh, ox, y, z, c)
    place = 2 * xh + xl
    x_up, x_down = lax.rem(place + 1, 4), lax.rem(place + 3, 4)
    x_right = dev(x_up // 2, lax.rem(x_up, 2), y, z, c)
    x_left = dev(x_down // 2, lax.rem(x_down, 2), y, z, c)

    own_loads = [
        pltpu.make_async_copy(go_hbm, go_v, local_sem.at[4]),
        pltpu.make_async_copy(taps_hbm, taps_v, local_sem.at[5]),
        pltpu.make_async_copy(tok_hbm, tokb.at[xh, y, c], local_sem.at[6]),
    ]
    for load in own_loads:
        load.start()
    barrier = pltpu.get_barrier_semaphore()
    peers = [sibling] + [along("y")(by) for by in (-2, -1, 1, 2)]
    peers += [along("z")(by) for by in range(1, 8)]
    for by in range(1, 4):
        other = lax.rem(place + by, 4)
        peers.append(dev(other // 2, lax.rem(other, 2), y, z, c))
    for peer in peers:
        pl.semaphore_signal(barrier, inc=1, device_id=peer, device_id_type=MESH)

    loads = [
        pltpu.make_async_copy(w_hbm, w_v, local_sem.at[0]),
        pltpu.make_async_copy(f_hbm, f_v, local_sem.at[1]),
        pltpu.make_async_copy(g_hbm, g_v, local_sem.at[2]),
        pltpu.make_async_copy(ct_hbm, ct_v, local_sem.at[3]),
    ]
    for load in loads:
        load.start()

    lane = lax.broadcasted_iota(jnp.int32, (64, 128), 1)
    low64 = lane < 64
    low128 = lax.broadcasted_iota(jnp.int32, (128, 128), 1) < 64

    def flip(v):
        return pltpu.roll(v, 64, 1)

    def fold_low(v, h):
        top, bottom = v[:64], v[64:]
        return jnp.where(low64, top, flip(bottom)) if h == 0 else jnp.where(low64, flip(top), bottom)

    def fold_high(v, h):
        top, bottom = v[:64], v[64:]
        return jnp.where(low64, bottom, flip(top)) if h == 0 else jnp.where(low64, flip(bottom), top)

    for load in own_loads:
        load.wait()
    go = go_v[...].astype(F32)
    taps = taps_v[...]
    packs = [
        jnp.concatenate([fold_high(go, h), fold_low(taps, h)], axis=0).astype(BF16)
        for h in range(2)
    ]
    first = xl == 0
    gtb[z, xl] = jnp.where(first, packs[0], packs[1])
    gtx[...] = jnp.where(first, packs[1], packs[0])

    pl.semaphore_wait(barrier, len(peers))

    tok_a = Spread(lambda q: tokb.at[xh, q, c], 128, y, along("y"), spread_s.at[0], tok_a_r)
    tok_b = Spread(lambda q: tokb.at[oh, q, c], 128, y, along("y"), spread_s.at[1], tok_b_r)
    gate_a = Spread(lambda q: gtb.at[q, xl], 128, z, along("z"), spread_s.at[2], gate_a_r)
    gate_b = Spread(lambda q: gtb.at[q, ox], 128, z, along("z"), spread_s.at[3], gate_b_r)
    proj_a = Spread(lambda q: qvb.at[q, xl], 192, z, along("z"), spread_s.at[4], proj_a_r)
    proj_b = Spread(lambda q: qvb.at[q, ox], 192, z, along("z"), spread_s.at[5], proj_b_r)

    total = w_v.at[0]
    index_of = {0: 0, -1: 1, -2: 2, -3: 3, -4: 4, 3: 5, 2: 6, 1: 7}

    def sib_copy(ref, group):
        return remote(ref, ref, sib_s.at[0], sib_r.at[group], sibling)

    def to_sibling(side, aways, group):
        for away in aways:
            sib_copy(tokb.at[xh if side == 0 else oh, turn(y, away), c], group).start()

    def from_sibling(pieces, group):
        sib_copy(total.at[pl.ds(0, 128 * pieces)], group).wait_recv()

    tok_pair_out = remote(tokb.at[xh, y, c], tokb.at[xh, y, c], pair_s.at[0], pair_r.at[0], h_partner)
    tok_pair_in = remote(tokb.at[oh, y, c], tokb.at[oh, y, c], pair_s.at[0], pair_r.at[0], h_partner)
    gate_out = remote(gtx, gtb.at[z, xl], pair_s.at[1], pair_r.at[1], l_partner)
    gate_in = remote(gtx, gtb.at[z, ox], pair_s.at[1], pair_r.at[1], l_partner)
    proj_out = remote(qvx, qvb.at[z, xl], pair_s.at[2], pair_r.at[2], l_partner)
    proj_in = remote(qvx, qvb.at[z, ox], pair_s.at[2], pair_r.at[2], l_partner)

    def turn_copy(away):
        q = turn(y, away)
        return remote(
            tokb.at[xh, q, c], tb.at[xh, c, xl, z], tr_s.at[0], tr_r.at[0], dev(xh, xl, y, q, c)
        )

    def turned_over(aways):
        for away in aways:
            q = turn(y, away)

            @pl.when(q == z)
            def _():
                tb[xh, c, xl, z] = tokb[xh, q, c]

            @pl.when(q != z)
            def _():
                turn_copy(away).start()

    def project(aways):
        summed = None
        for away in aways:
            for side in range(2):
                q = turn(y, away)
                h = xh if side == 0 else oh
                left = jnp.concatenate([tokb[h, q, 0], tokb[h, q, 1]], axis=1)
                rows = pl.ds(pl.multiple_of((h * 8 + q) * 256, 256), 256)
                right = jnp.concatenate([w_v[j, rows, :] for j in range(3)], axis=1)
                term = jnp.dot(left, right, preferred_element_type=F32)
                summed = term if summed is None else summed + term
        return summed

    tok_pair_out.start()
    tok_a.first()
    to_sibling(0, [0], 0)
    gate_out.start()
    gate_a.first()
    turned_over([0])
    tok_pair_in.wait_recv()
    tok_b.first()
    to_sibling(1, [0], 0)
    gate_in.wait_recv()
    gate_b.first()
    loads[0].wait()
    near, far = [-2, 2, -1, 1], [-3, 3, -4]
    tok_a.middle(total)
    to_sibling(0, near, 1)
    turned_over(near)
    from_sibling(2, 0)
    acc[...] = project([0])
    tok_b.middle(total)
    to_sibling(1, near, 1)
    tok_a.last(total)
    to_sibling(0, far, 2)
    turned_over(far)
    gate_a.middle(total)
    gate_b.middle(total)
    from_sibling(8, 1)
    acc[...] += project(near)
    tok_b.last(total)
    to_sibling(1, far, 2)
    from_sibling(6, 2)
    projected = (acc[...] + project(far)).astype(BF16).astype(F32)

    qp, kp, vp = projected[:, :128], projected[:, 128:256], projected[:, 256:]
    both = []
    for h in range(2):
        kq = jnp.where(low128, kp, flip(qp)) if h == 0 else jnp.where(low128, flip(kp), qp)
        both.append(jnp.concatenate([kq, fold_low(vp, h)], axis=0).astype(BF16))
    qvx[...] = jnp.where(first, both[1], both[0])
    proj_out.start()
    qvb[z, xl] = jnp.where(first, both[0], both[1])
    proj_a.first()


    up_h, up_l = x_up // 2, lax.rem(x_up, 2)
    down_h, down_l = x_down // 2, lax.rem(x_down, 2)

    def block_of(h, core, l, k):
        return tb.at[h, core, l, pl.ds(PER * k, PER)]

    def along_x(way, k):
        ref = block_of(xh, c, xl, k)
        return remote(ref, ref, tx_s.at[0], tx_r.at[way, k], x_right if way == 0 else x_left)

    def from_x(way, k):
        ref = block_of(down_h, c, down_l, k) if way == 0 else block_of(up_h, c, up_l, k)
        return remote(ref, ref, tx_s.at[0], tx_r.at[way, k], x_right if way == 0 else x_left)

    def half_on(way, k):
        h, l = (down_h, down_l) if way == 0 else (up_h, up_l)
        ref = tb.at[h, c, l, pl.ds(PER * k + PER // 2 * way, PER // 2)]
        return remote(ref, ref, tx_s.at[0], tx2_r.at[k], x_right if way == 0 else x_left)

    def across(k):
        ref = block_of(oh, c, xl, k)
        return remote(ref, ref, tx_s.at[0], tx2_r.at[k], x_right)

    piece_at = [(xh, xl), (down_h, down_l), (up_h, up_l), (oh, xl)]

    def t_sibling(piece, k, core):
        h, l = piece_at[piece]
        ref = block_of(h, core, l, k)
        return remote(ref, ref, ts_s.at[0], ts_r.at[0], sibling)

    def count(s, r, rows):
        ref = total.at[pl.ds(0, rows)]
        return remote(ref, ref, s, r, sibling)

    def round_x_first():
        count(tr_s.at[0], tr_r.at[0], 7 * 128).wait_recv()
        for k in range(CHUNKS):
            along_x(0, k).start()
            along_x(1, k).start()
            t_sibling(0, k, c).start()

    def round_x_second():
        for k in range(CHUNKS):
            from_x(0, k).wait_recv()
            half_on(0, k).start()
            from_x(1, k).wait_recv()
            half_on(1, k).start()
            t_sibling(1, k, c).start()
            t_sibling(2, k, c).start()

    def round_x_third():
        for k in range(CHUNKS):
            across(k).wait_recv()
            t_sibling(3, k, c).start()

    round_x_first()
    proj_in.wait_recv()
    proj_b.first()
    gate_a.last(total)
    gate_b.last(total)


    def put_spectra(x, rows_lo, rows_hi):
        spectra = real_forward(32, x)
        yb[0, rows_lo, :] = spectra[0][0].astype(BF16)
        yb[0, rows_hi, :] = spectra[16][0].astype(BF16)
        for k in range(1, 16):
            yb[k, rows_lo, :] = spectra[k][0].astype(BF16)
            yb[k, rows_hi, :] = spectra[k][1].astype(BF16)

    low16 = lax.broadcasted_iota(jnp.int32, (16, 128), 1) < 64

    def rows_at(start):
        return pl.ds(pl.multiple_of(start, 16), 16)

    def filter_rows(i, carry):
        top, bottom = [], []
        for a in range(16):
            packed = gtb[a % 8, a // 8, rows_at(64 + 16 * i), :].astype(F32)
            turned = flip(packed)
            top.append(jnp.where(low16, packed, turned))
            bottom.append(jnp.where(low16, turned, packed))
        put_spectra(top, rows_at(16 * i), rows_at(128 + 16 * i))
        put_spectra(bottom, rows_at(64 + 16 * i), rows_at(192 + 16 * i))
        return carry

    lax.fori_loop(0, 4, filter_rows, 0)
    loads[1].wait()
    row0 = lax.broadcasted_iota(jnp.int32, (128, 128), 0) == 0

    def filter_tile(k, carry):
        spec = jnp.dot(f_v[k], yb[k], preferred_element_type=F32)
        fs[k, :128, :] = spec[:128]
        im = spec[128:]
        special = jnp.logical_and(row0, k == 0)
        fs[k, 128:, :] = jnp.where(jnp.logical_or(low128, special), im, -im)
        return carry

    lax.fori_loop(0, 16, filter_tile, 0, unroll=16)

    proj_a.middle(total)
    proj_b.middle(total)
    round_x_second()
    proj_a.last(total)
    proj_b.last(total)


    def field_rows(i, carry):
        top, bottom = [], []
        for a in range(16):
            za, la = a % 8, a // 8
            vals = qvb[za, la, rows_at(128 + 16 * i), :].astype(F32)
            gos = gtb[za, la, rows_at(16 * i), :].astype(F32)
            b_top = jnp.where(low16, vals, gos)
            b_bottom = flip(jnp.where(low16, gos, vals))
            bv[a, rows_at(16 * i), :] = b_top.astype(BF16)
            bv[a, rows_at(64 + 16 * i), :] = b_bottom.astype(BF16)
            top.append(qvb[za, la, rows_at(16 * i), :].astype(F32) * b_top)
            bottom.append(qvb[za, la, rows_at(64 + 16 * i), :].astype(F32) * b_bottom)
        put_spectra(top, rows_at(16 * i), rows_at(128 + 16 * i))
        put_spectra(bottom, rows_at(64 + 16 * i), rows_at(192 + 16 * i))
        return carry

    lax.fori_loop(0, 4, field_rows, 0, unroll=4)
    round_x_third()
    loads[2].wait()

    def mix_tile(k, carry):
        spec = jnp.dot(f_v[k], yb[k], preferred_element_type=F32)
        sr, si = spec[:128], spec[128:]
        fr, fi = fs[k, :128, :], fs[k, 128:, :]
        tr, ti = flip(sr), flip(si)
        special = jnp.logical_and(row0, k == 0)
        mixed_re = jnp.where(special, fr * sr, fr * sr - fi * si)
        mixed_im = jnp.where(special, fi * si, fr * si + fi * sr)
        grad_re = jnp.where(special, tr * sr, tr * sr + ti * si)
        grad_im = jnp.where(special, ti * si, ti * sr - tr * si)
        mixed = jnp.concatenate([mixed_re, mixed_im], axis=0).astype(BF16)
        zb[k] = jnp.dot(g_v[k], mixed, preferred_element_type=F32)
        yb[k] = jnp.concatenate([grad_re, grad_im], axis=0).astype(BF16)
        return carry

    lax.fori_loop(0, 16, mix_tile, 0, unroll=16)


    def back_rows(i, carry):
        lo, hi = rows_at(16 * i), rows_at(128 + 16 * i)
        spectra = [(zb[0, lo, :], None)]
        spectra += [(zb[k, lo, :], zb[k, hi, :]) for k in range(1, 16)]
        spectra += [(zb[0, hi, :], None)]
        for a, restored in enumerate(real_inverse(32, spectra, half=True)):
            turned = flip(restored)
            out = rows_at(128 * a + 16 * i)
            gp[out, :128] = (turned * bv[a, lo, :].astype(F32)).astype(BF16)
            gp[out, 128:] = (turned * qvb[a % 8, a // 8, lo, :].astype(F32)).astype(BF16)
        return carry

    lax.fori_loop(0, 8, back_rows, 0, unroll=2)


    count(ts_s.at[0], ts_r.at[0], 4096).wait_recv()

    def weight_rows(h, core):
        lhs = tb[h, core].reshape(2048, 128)
        return lax.dot_general(lhs, gp[...], (((0,), (0,)), ((), ())), preferred_element_type=F32)

    away_parts = [weight_rows(ox, core) for core in range(2)]
    for core in range(2):
        rsend[core * 128 : core * 128 + 128, :] = away_parts[core][:, :128].astype(BF16)
    rsend[256:, :] = jnp.where(low128, away_parts[0][:, 128:], flip(away_parts[1][:, 128:])).astype(BF16)
    weight_out = remote(rsend, rrecv, pair_s.at[3], pair_r.at[3], l_partner)
    weight_out.start()

    loads[3].wait()

    def filter_grad_step(k, carry):
        sums = []
        back = jnp.dot(g_v[k], yb[k], preferred_element_type=F32)
        for l in range(2):
            block = z + 8 * l
            total = carry[l] + ct_v[block, pl.ds(k, 1), :] * back[:128]
            sums.append(total + ct_v[block, pl.ds(k + 16, 1), :] * back[128:])
        return tuple(sums)

    zero = jnp.zeros((128, 128), F32)
    near, far = lax.fori_loop(0, 16, filter_grad_step, (zero, zero), unroll=16)
    own = jnp.where(first, near, far)
    other = jnp.where(first, far, near)
    fsend[...] = jnp.where(low64, other[:64], flip(other[64:]))
    filter_out = remote(fsend, frecv, pair_s.at[4], pair_r.at[4], l_partner)
    filter_out.start()
    fown[...] = own

    for core in range(2):
        rown[core * 128 : core * 128 + 128, :] = weight_rows(xl, core)

    def unfolded(mine, got):
        turned, turned_mine = flip(got), flip(mine)
        low = lax.broadcasted_iota(jnp.int32, mine.shape, 1) < 64
        as_first = jnp.where(low, mine, jnp.concatenate([turned, got], axis=0))
        as_second = jnp.where(low, jnp.concatenate([got, turned], axis=0), turned_mine)
        return jnp.where(first, as_first, as_second)

    weight_out.wait_recv()
    mine = rown[:, :128]
    got = rrecv[:256, :].astype(F32)
    mine_turned, got_turned = flip(mine), flip(got)
    low256 = lax.broadcasted_iota(jnp.int32, (256, 128), 1) < 64
    wg_ref[0] = jnp.where(
        first, jnp.where(low256, mine_turned, got), jnp.where(low256, got_turned, mine)
    )
    wg_ref[1] = jnp.where(
        first, jnp.where(low256, mine, got_turned), jnp.where(low256, got, mine_turned)
    )
    wg_ref[2] = unfolded(rown[:, 128:], rrecv[256:, :].astype(F32))
    filter_out.wait_recv()
    fg_ref[...] = unfolded(fown[...], frecv[...])

    for spread in (tok_a, tok_b, gate_a, gate_b, proj_a, proj_b):
        spread.drain(total)
    for sent in (tok_pair_out, gate_out, proj_out, weight_out, filter_out):
        sent.wait_send()
    for s, rows in ((sib_s, 16 * 128), (tr_s, 7 * 128), (tx_s, 3072), (ts_s, 4096)):
        count(s.at[0], sib_r.at[0], rows).wait_send()


def on_device(tables, tokens, in_weight, filter_taps, grad_out):
    forward, inverse, single = tables
    vmem = pl.BlockSpec(memory_space=pltpu.VMEM)
    anywhere = pl.BlockSpec(memory_space=pltpu.HBM)
    dma = pltpu.SemaphoreType.DMA
    weight_grad, filter_grad = pl.pallas_call(
        kernel,
        out_shape=(
            jax.ShapeDtypeStruct((3, 256, 128), F32),
            jax.ShapeDtypeStruct((128, 128), F32),
        ),
        in_specs=[anywhere] * 7,
        out_specs=(vmem, vmem),
        scratch_shapes=[
            pltpu.VMEM((128, 128), BF16),
            pltpu.VMEM((128, 128), F32),
            pltpu.VMEM((3, 4096, 128), BF16),
            pltpu.VMEM((16, 256, 256), BF16),
            pltpu.VMEM((16, 256, 256), BF16),
            pltpu.VMEM((16, 32, 128), F32),
            pltpu.VMEM((2, 8, 2, 128, 128), BF16),
            pltpu.VMEM((8, 2, 128, 128), BF16),
            pltpu.VMEM((128, 128), BF16),
            pltpu.VMEM((8, 2, 192, 128), BF16),
            pltpu.VMEM((192, 128), BF16),
            pltpu.VMEM((2, 2, 2, 8, 128, 128), BF16),
            pltpu.VMEM((128, 384), F32),
            pltpu.VMEM((16, 128, 128), BF16),
            pltpu.VMEM((16, 256, 128), BF16),
            pltpu.VMEM((16, 256, 128), F32),
            pltpu.VMEM((16, 256, 128), F32),
            pltpu.VMEM((2048, 256), BF16),
            pltpu.VMEM((256, 256), F32),
            pltpu.VMEM((384, 128), BF16),
            pltpu.VMEM((384, 128), BF16),
            pltpu.VMEM((128, 128), F32),
            pltpu.VMEM((64, 128), F32),
            pltpu.VMEM((64, 128), F32),
            dma((7,)),
            dma((6,)),
            *[dma((4,)) for _ in range(6)],
            dma((5,)), dma((5,)),
            dma((1,)), dma((3,)),
            dma((1,)), dma((1,)),
            dma((1,)), dma((2, CHUNKS)), dma((CHUNKS,)),
            dma((1,)), dma((1,)),
        ],
        compiler_params=pltpu.CompilerParams(
            collective_id=0, has_side_effects=True, vmem_limit_bytes=52 * 1024 * 1024
        ),
        cost_estimate=pl.CostEstimate(flops=3_000_000_000, bytes_accessed=10_000_000, transcendentals=0),
    )(
        *[
            pltpu.with_memory_space_constraint(operand, pltpu.HBM)
            for operand in (
                tokens, grad_out, filter_taps, jnp.transpose(in_weight, (1, 0, 2)), forward, inverse, single
            )
        ]
    )
    return jnp.transpose(weight_grad, (1, 0, 2)), filter_grad


def solution(mesh):
    tables = transform_tables()

    def whole(tokens, in_weight, filter_taps, grad_out):
        constants = tuple(jnp.asarray(t) for t in tables)
        placed = (P("ctx", "ch"), P(None, None, "ch"), P("ctx", "ch"), P("ctx", "ch"))
        return jax.shard_map(
            on_device,
            mesh=mesh,
            in_specs=((P(), P(), P()),) + placed,
            out_specs=(P("ctx", None, "ch"), P("ctx", "ch")),
            check_vma=False,
        )(constants, tokens, in_weight, filter_taps, grad_out)

    return whole
```

```python
import math

import jax
import jax.numpy as jnp
import ml_dtypes
import numpy as np
from jax import lax
from jax.experimental import pallas as pl
from jax.experimental.pallas import tpu as pltpu
from jax.sharding import PartitionSpec as P

MESH = pl.DeviceIdType.MESH
BF16 = jnp.bfloat16
F32 = jnp.float32
ROWS = 128
TILES = 16
CHUNKS = 2
PER = 8 // CHUNKS


def transform_tables():
    r = np.arange(128)
    k1 = np.arange(128)
    forward = np.zeros((16, 256, 256))
    inverse = np.zeros((16, 256, 256))
    for k2 in range(1, 16):
        angle = 2 * np.pi * (((k2 + 32 * k1)[:, None] * r[None, :]) % 4096) / 4096
        c, s = np.cos(angle), np.sin(angle)
        forward[k2] = np.block([[c, s], [-s, c]])
        inverse[k2] = np.block([[c.T, -s.T], [s.T, c.T]]) * (2 / 4096)
    k1 = np.arange(64)
    a0 = 2 * np.pi * ((32 * k1[:, None] * r[None, :]) % 4096) / 4096
    a16 = 2 * np.pi * (((16 + 32 * k1)[:, None] * r[None, :]) % 4096) / 4096
    nyquist = 1.0 - 2.0 * (r % 2)
    re0, im0 = np.cos(a0), -np.sin(a0)
    im0[0] = nyquist
    zero = np.zeros((64, 128))
    forward[0] = np.block(
        [
            [re0, zero],
            [zero, np.cos(a16)],
            [im0, zero],
            [zero, -np.sin(a16)],
        ]
    )
    back_re0, back_im0 = 2 * np.cos(a0).T, -2 * np.sin(a0).T
    back_re0[:, 0] = 1.0
    back_im0[:, 0] = nyquist
    zero = np.zeros((128, 64))
    inverse[0] = (
        np.block(
            [
                [back_re0, zero, back_im0, zero],
                [zero, 2 * np.cos(a16).T, zero, -2 * np.sin(a16).T],
            ]
        )
        / 4096
    )
    block = np.arange(16)[:, None]
    k = np.arange(16)[None, :]
    angle = 2 * np.pi * ((block * k) % 32) / 32
    im_part = -np.sin(angle)
    im_part[:, 0] = 1.0 - 2.0 * (np.arange(16) % 2)
    single = np.concatenate([np.cos(angle), im_part], axis=1)
    single = np.broadcast_to(single[:, :, None], (16, 32, 128))
    return (
        forward.astype(ml_dtypes.bfloat16),
        inverse.astype(ml_dtypes.bfloat16),
        single.astype(np.float32),
    )


def root(n, a, sign):
    angle = -sign * 2 * math.pi * a / n
    return math.cos(angle), math.sin(angle)


def times(v, w):
    re, im = v
    wr, wi = w
    if abs(wi) < 1e-12:
        return (re, im) if wr > 0 else (-re, -im)
    if abs(wr) < 1e-12:
        return (-im, re) if wi > 0 else (im, -re)
    return re * wr - im * wi, re * wi + im * wr


def complex_dft(u, sign):
    n = len(u)
    if n == 1:
        return u
    h = n // 2
    low = [(u[a][0] + u[a + h][0], u[a][1] + u[a + h][1]) for a in range(h)]
    high = [
        times((u[a][0] - u[a + h][0], u[a][1] - u[a + h][1]), root(n, a, sign))
        for a in range(h)
    ]
    even, odd = complex_dft(low, sign), complex_dft(high, sign)
    return [even[i // 2] if i % 2 == 0 else odd[i // 2] for i in range(n)]


def real_forward(n, x):
    if n == 2:
        return [(x[0] + x[1], None), (x[0] - x[1], None)]
    h, q = n // 2, n // 4
    if len(x) == h:
        fold, diff = x, x
    else:
        fold = [x[a] + x[a + h] for a in range(h)]
        diff = [x[a] - x[a + h] for a in range(h)]
    even = real_forward(h, fold)
    odd = complex_dft(
        [times((diff[a], -diff[a + q]), root(n, a, 1)) for a in range(q)], 1
    )
    out = [None] * (h + 1)
    for m in range(h // 2 + 1):
        out[2 * m] = even[m]
    for j in range(q):
        k = 4 * j + 1
        if k <= h:
            out[k] = odd[j]
        else:
            out[n - k] = (odd[j][0], -odd[j][1])
    return out


def real_inverse(n, z, half=False):
    if n == 2:
        return [z[0][0] + z[1][0], z[0][0] - z[1][0]]
    h, q = n // 2, n // 4
    even = real_inverse(h, z[0::2])
    v = []
    for j in range(q):
        k = 4 * j + 1
        v.append(z[k] if k <= h else (z[n - k][0], -z[n - k][1]))
    s = complex_dft(v, -1)
    t = [times(s[a], root(n, a, -1)) for a in range(q)]
    odd = [t[a][0] for a in range(q)] + [-t[a][1] for a in range(q)]
    low = [even[a] + odd[a] for a in range(h)]
    return low if half else low + [even[a] - odd[a] for a in range(h)]


class Spread:
    def __init__(self, slot, rows, place, to, send_sem, recv_sem):
        self.slot, self.rows, self.place, self.to = slot, rows, place, to
        self.send_sem, self.recv_sem = send_sem, recv_sem
        self.sent = 0

    def piece(self, origin):
        return self.slot(lax.rem(self.place + 8 + origin, 8))

    def copy(self, ref, seen, device):
        at = {-2: 0, 2: 1, -1: 2, 1: 2}.get(seen, 3)
        return pltpu.make_async_remote_copy(
            src_ref=ref, dst_ref=ref, send_sem=self.send_sem, recv_sem=self.recv_sem.at[at],
            device_id=device, device_id_type=MESH,
        )

    def send(self, origin, distance, half=None):
        ref, rows = self.piece(origin), self.rows
        if half is not None:
            rows = rows // 2
            ref = ref.at[pl.ds(half * rows, rows)]
        self.copy(ref, origin - distance, self.to(distance)).start()
        self.sent += rows

    def wait(self, pieces, seen, total):
        self.copy(total.at[pl.ds(0, pieces * self.rows)], seen, self.to(1)).wait_recv()

    def first(self):
        for distance in (2, -2, 1, -1):
            self.send(0, distance)

    def middle(self, total):
        self.wait(1, -2, total)
        self.send(-2, 2, 0)
        self.send(-2, 1)
        self.wait(1, 2, total)
        self.send(2, -2, 1)
        self.send(2, -1)
        self.wait(2, 1, total)

    def last(self, total):
        self.wait(3, 3, total)

    def drain(self, total):
        self.copy(total.at[pl.ds(0, self.sent)], 1, self.to(1)).wait_send()


def kernel(
    tok_hbm, go_hbm, taps_hbm, w_hbm, f_hbm, g_hbm, ct_hbm,
    wg_ref, fg_ref,
    go_v, taps_v, w_v, f_v, g_v, ct_v, tokb, gtb, gtx, qvb, qvx, tb, acc, bv, yb, fs, zb, gp,
    rown, rsend, rrecv, fown, fsend, frecv,
    local_sem, spread_s, tok_a_r, tok_b_r, gate_a_r, gate_b_r, proj_a_r, proj_b_r,
    pair_s, pair_r, sib_s, sib_r, tr_s, tr_r, tx_s, tx_r, tx2_r, ts_s, ts_r,
):
    ctx, ch = lax.axis_index("ctx"), lax.axis_index("ch")
    xl, z = ctx // 8, lax.rem(ctx, 8)
    c, xh, y = lax.rem(ch, 2), ch // 16, lax.rem(ch // 2, 8)
    ox, oh, oc = 1 - xl, 1 - xh, 1 - c

    def dev(xh_, xl_, y_, z_, c_):
        return (xl_ * 8 + z_, (xh_ * 8 + y_) * 2 + c_)

    def remote(src, dst, s, r, to):
        return pltpu.make_async_remote_copy(
            src_ref=src, dst_ref=dst, send_sem=s, recv_sem=r, device_id=to, device_id_type=MESH
        )

    def turn(v, by):
        return lax.rem(v + 8 + by, 8)

    def along(axis):
        if axis == "y":
            return lambda by: dev(xh, xl, turn(y, by), z, c)
        return lambda by: dev(xh, xl, y, turn(z, by), c)

    sibling = dev(xh, xl, y, z, oc)
    h_partner = dev(oh, xl, y, z, c)
    l_partner = dev(xh, ox, y, z, c)
    place = 2 * xh + xl
    x_up, x_down = lax.rem(place + 1, 4), lax.rem(place + 3, 4)
    x_right = dev(x_up // 2, lax.rem(x_up, 2), y, z, c)
    x_left = dev(x_down // 2, lax.rem(x_down, 2), y, z, c)

    own_loads = [
        pltpu.make_async_copy(go_hbm, go_v, local_sem.at[4]),
        pltpu.make_async_copy(taps_hbm, taps_v, local_sem.at[5]),
        pltpu.make_async_copy(tok_hbm, tokb.at[c, y, xh], local_sem.at[6]),
    ]
    for load in own_loads:
        load.start()
    barrier = pltpu.get_barrier_semaphore()
    peers = [sibling] + [along("y")(by) for by in (-2, -1, 1, 2)]
    peers += [along("z")(by) for by in range(1, 8)]
    for by in range(1, 4):
        other = lax.rem(place + by, 4)
        peers.append(dev(other // 2, lax.rem(other, 2), y, z, c))
    for peer in peers:
        pl.semaphore_signal(barrier, inc=1, device_id=peer, device_id_type=MESH)

    loads = [
        pltpu.make_async_copy(w_hbm, w_v, local_sem.at[0]),
        pltpu.make_async_copy(f_hbm, f_v, local_sem.at[1]),
        pltpu.make_async_copy(g_hbm, g_v, local_sem.at[2]),
        pltpu.make_async_copy(ct_hbm, ct_v, local_sem.at[3]),
    ]
    for load in loads:
        load.start()

    lane = lax.broadcasted_iota(jnp.int32, (64, 128), 1)
    low64 = lane < 64
    low128 = lax.broadcasted_iota(jnp.int32, (128, 128), 1) < 64

    def flip(v):
        return pltpu.roll(v, 64, 1)

    def fold_low(v, h):
        top, bottom = v[:64], v[64:]
        return jnp.where(low64, top, flip(bottom)) if h == 0 else jnp.where(low64, flip(top), bottom)

    def fold_high(v, h):
        top, bottom = v[:64], v[64:]
        return jnp.where(low64, bottom, flip(top)) if h == 0 else jnp.where(low64, flip(bottom), top)

    for load in own_loads:
        load.wait()
    go = go_v[...].astype(F32)
    taps = taps_v[...]
    packs = [
        jnp.concatenate([fold_high(go, h), fold_low(taps, h)], axis=0).astype(BF16)
        for h in range(2)
    ]
    first = xl == 0
    gtb[z, xl] = jnp.where(first, packs[0], packs[1])
    gtx[...] = jnp.where(first, packs[1], packs[0])

    pl.semaphore_wait(barrier, len(peers))

    tok_a = Spread(lambda q: tokb.at[c, q, xh], 128, y, along("y"), spread_s.at[0], tok_a_r)
    tok_b = Spread(lambda q: tokb.at[c, q, oh], 128, y, along("y"), spread_s.at[1], tok_b_r)
    gate_a = Spread(lambda q: gtb.at[q, xl], 128, z, along("z"), spread_s.at[2], gate_a_r)
    gate_b = Spread(lambda q: gtb.at[q, ox], 128, z, along("z"), spread_s.at[3], gate_b_r)
    proj_a = Spread(lambda q: qvb.at[q, xl], 192, z, along("z"), spread_s.at[4], proj_a_r)
    proj_b = Spread(lambda q: qvb.at[q, ox], 192, z, along("z"), spread_s.at[5], proj_b_r)

    total = w_v.at[0]
    index_of = {0: 0, -1: 1, -2: 2, -3: 3, -4: 4, 3: 5, 2: 6, 1: 7}

    def sib_copy(ref, group):
        return remote(ref, ref, sib_s.at[0], sib_r.at[group], sibling)

    def to_sibling(aways, group):
        for away in aways:
            sib_copy(tokb.at[c, turn(y, away)], group).start()

    def from_sibling(pieces, group):
        sib_copy(total.at[pl.ds(0, 128 * pieces)], group).wait_recv()

    tok_pair_out = remote(tokb.at[c, y, xh], tokb.at[c, y, xh], pair_s.at[0], pair_r.at[0], h_partner)
    tok_pair_in = remote(tokb.at[c, y, oh], tokb.at[c, y, oh], pair_s.at[0], pair_r.at[0], h_partner)
    gate_out = remote(gtx, gtb.at[z, xl], pair_s.at[1], pair_r.at[1], l_partner)
    gate_in = remote(gtx, gtb.at[z, ox], pair_s.at[1], pair_r.at[1], l_partner)
    proj_out = remote(qvx, qvb.at[z, xl], pair_s.at[2], pair_r.at[2], l_partner)
    proj_in = remote(qvx, qvb.at[z, ox], pair_s.at[2], pair_r.at[2], l_partner)

    def turn_copy(away):
        q = turn(y, away)
        return remote(
            tokb.at[c, q, xh], tb.at[xh, c, xl, z], tr_s.at[0], tr_r.at[0], dev(xh, xl, y, q, c)
        )

    def turned_over(aways):
        for away in aways:
            q = turn(y, away)

            @pl.when(q == z)
            def _():
                tb[xh, c, xl, z] = tokb[c, q, xh]

            @pl.when(q != z)
            def _():
                turn_copy(away).start()

    def project(aways):
        summed = None
        for away in aways:
            for side in range(2):
                q = turn(y, away)
                h = xh if side == 0 else oh
                left = jnp.concatenate([tokb[0, q, h], tokb[1, q, h]], axis=1)
                rows = pl.ds(pl.multiple_of((h * 8 + q) * 256, 256), 256)
                right = jnp.concatenate([w_v[j, rows, :] for j in range(3)], axis=1)
                term = jnp.dot(left, right, preferred_element_type=F32)
                summed = term if summed is None else summed + term
        return summed

    tok_pair_out.start()
    tok_a.first()
    gate_out.start()
    gate_a.first()
    turned_over([0])
    tok_pair_in.wait_recv()
    tok_b.first()
    to_sibling([0], 0)
    gate_in.wait_recv()
    gate_b.first()
    loads[0].wait()
    near, far = [-2, 2, -1, 1], [-3, 3, -4]
    tok_a.middle(total)
    turned_over(near)
    from_sibling(2, 0)
    acc[...] = project([0])
    tok_b.middle(total)
    to_sibling(near, 1)
    tok_a.last(total)
    turned_over(far)
    gate_a.middle(total)
    gate_b.middle(total)
    from_sibling(8, 1)
    acc[...] += project(near)
    tok_b.last(total)
    to_sibling(far, 2)
    from_sibling(6, 2)
    projected = (acc[...] + project(far)).astype(BF16).astype(F32)

    qp, kp, vp = projected[:, :128], projected[:, 128:256], projected[:, 256:]
    both = []
    for h in range(2):
        kq = jnp.where(low128, kp, flip(qp)) if h == 0 else jnp.where(low128, flip(kp), qp)
        both.append(jnp.concatenate([kq, fold_low(vp, h)], axis=0).astype(BF16))
    qvx[...] = jnp.where(first, both[1], both[0])
    proj_out.start()
    qvb[z, xl] = jnp.where(first, both[0], both[1])
    proj_a.first()


    up_h, up_l = x_up // 2, lax.rem(x_up, 2)
    down_h, down_l = x_down // 2, lax.rem(x_down, 2)

    def block_of(h, core, l, k):
        return tb.at[h, core, l, pl.ds(PER * k, PER)]

    def along_x(way, k):
        ref = block_of(xh, c, xl, k)
        return remote(ref, ref, tx_s.at[0], tx_r.at[way, k], x_right if way == 0 else x_left)

    def from_x(way, k):
        ref = block_of(down_h, c, down_l, k) if way == 0 else block_of(up_h, c, up_l, k)
        return remote(ref, ref, tx_s.at[0], tx_r.at[way, k], x_right if way == 0 else x_left)

    def half_on(way, k):
        h, l = (down_h, down_l) if way == 0 else (up_h, up_l)
        ref = tb.at[h, c, l, pl.ds(PER * k + PER // 2 * way, PER // 2)]
        return remote(ref, ref, tx_s.at[0], tx2_r.at[k], x_right if way == 0 else x_left)

    def across(k):
        ref = block_of(oh, c, xl, k)
        return remote(ref, ref, tx_s.at[0], tx2_r.at[k], x_right)

    piece_at = [(xh, xl), (down_h, down_l), (up_h, up_l), (oh, xl)]

    def t_sibling(piece, k, core):
        h, l = piece_at[piece]
        ref = block_of(h, core, l, k)
        return remote(ref, ref, ts_s.at[0], ts_r.at[0], sibling)

    def count(s, r, rows):
        ref = total.at[pl.ds(0, rows)]
        return remote(ref, ref, s, r, sibling)

    def round_x_first():
        count(tr_s.at[0], tr_r.at[0], 7 * 128).wait_recv()
        for k in range(CHUNKS):
            along_x(0, k).start()
            along_x(1, k).start()
            t_sibling(0, k, c).start()

    def round_x_second():
        for k in range(CHUNKS):
            from_x(0, k).wait_recv()
            half_on(0, k).start()
            from_x(1, k).wait_recv()
            half_on(1, k).start()
            t_sibling(1, k, c).start()
            t_sibling(2, k, c).start()

    def round_x_third():
        for k in range(CHUNKS):
            across(k).wait_recv()
            t_sibling(3, k, c).start()

    proj_in.wait_recv()
    proj_b.first()
    round_x_first()
    gate_a.last(total)
    gate_b.last(total)


    def put_spectra(x, rows_lo, rows_hi):
        spectra = real_forward(32, x)
        yb[0, rows_lo, :] = spectra[0][0].astype(BF16)
        yb[0, rows_hi, :] = spectra[16][0].astype(BF16)
        for k in range(1, 16):
            yb[k, rows_lo, :] = spectra[k][0].astype(BF16)
            yb[k, rows_hi, :] = spectra[k][1].astype(BF16)

    low16 = lax.broadcasted_iota(jnp.int32, (16, 128), 1) < 64

    def rows_at(start):
        return pl.ds(pl.multiple_of(start, 16), 16)

    def filter_rows(i, carry):
        top, bottom = [], []
        for a in range(16):
            packed = gtb[a % 8, a // 8, rows_at(64 + 16 * i), :].astype(F32)
            turned = flip(packed)
            top.append(jnp.where(low16, packed, turned))
            bottom.append(jnp.where(low16, turned, packed))
        put_spectra(top, rows_at(16 * i), rows_at(128 + 16 * i))
        put_spectra(bottom, rows_at(64 + 16 * i), rows_at(192 + 16 * i))
        return carry

    lax.fori_loop(0, 4, filter_rows, 0)
    loads[1].wait()
    row0 = lax.broadcasted_iota(jnp.int32, (128, 128), 0) == 0

    def filter_tile(k, carry):
        spec = jnp.dot(f_v[k], yb[k], preferred_element_type=F32)
        fs[k, :128, :] = spec[:128]
        im = spec[128:]
        special = jnp.logical_and(row0, k == 0)
        fs[k, 128:, :] = jnp.where(jnp.logical_or(low128, special), im, -im)
        return carry

    lax.fori_loop(0, 16, filter_tile, 0, unroll=16)

    proj_a.middle(total)
    proj_b.middle(total)
    round_x_second()
    proj_a.last(total)
    proj_b.last(total)


    def field_rows(i, carry):
        top, bottom = [], []
        for a in range(16):
            za, la = a % 8, a // 8
            vals = qvb[za, la, rows_at(128 + 16 * i), :].astype(F32)
            gos = gtb[za, la, rows_at(16 * i), :].astype(F32)
            b_top = jnp.where(low16, vals, gos)
            b_bottom = flip(jnp.where(low16, gos, vals))
            bv[a, rows_at(16 * i), :] = b_top.astype(BF16)
            bv[a, rows_at(64 + 16 * i), :] = b_bottom.astype(BF16)
            top.append(qvb[za, la, rows_at(16 * i), :].astype(F32) * b_top)
            bottom.append(qvb[za, la, rows_at(64 + 16 * i), :].astype(F32) * b_bottom)
        put_spectra(top, rows_at(16 * i), rows_at(128 + 16 * i))
        put_spectra(bottom, rows_at(64 + 16 * i), rows_at(192 + 16 * i))
        return carry

    lax.fori_loop(0, 4, field_rows, 0, unroll=4)
    round_x_third()
    loads[2].wait()

    def mix_tile(k, carry):
        spec = jnp.dot(f_v[k], yb[k], preferred_element_type=F32)
        sr, si = spec[:128], spec[128:]
        fr, fi = fs[k, :128, :], fs[k, 128:, :]
        tr, ti = flip(sr), flip(si)
        special = jnp.logical_and(row0, k == 0)
        mixed_re = jnp.where(special, fr * sr, fr * sr - fi * si)
        mixed_im = jnp.where(special, fi * si, fr * si + fi * sr)
        grad_re = jnp.where(special, tr * sr, tr * sr + ti * si)
        grad_im = jnp.where(special, ti * si, ti * sr - tr * si)
        mixed = jnp.concatenate([mixed_re, mixed_im], axis=0).astype(BF16)
        zb[k] = jnp.dot(g_v[k], mixed, preferred_element_type=F32)
        yb[k] = jnp.concatenate([grad_re, grad_im], axis=0).astype(BF16)
        return carry

    lax.fori_loop(0, 16, mix_tile, 0, unroll=16)


    def back_rows(i, carry):
        lo, hi = rows_at(16 * i), rows_at(128 + 16 * i)
        spectra = [(zb[0, lo, :], None)]
        spectra += [(zb[k, lo, :], zb[k, hi, :]) for k in range(1, 16)]
        spectra += [(zb[0, hi, :], None)]
        for a, restored in enumerate(real_inverse(32, spectra, half=True)):
            turned = flip(restored)
            out = rows_at(128 * a + 16 * i)
            gp[out, :128] = (turned * bv[a, lo, :].astype(F32)).astype(BF16)
            gp[out, 128:] = (turned * qvb[a % 8, a // 8, lo, :].astype(F32)).astype(BF16)
        return carry

    lax.fori_loop(0, 8, back_rows, 0, unroll=2)


    count(ts_s.at[0], ts_r.at[0], 4096).wait_recv()

    def weight_rows(h, core):
        lhs = tb[h, core].reshape(2048, 128)
        return lax.dot_general(lhs, gp[...], (((0,), (0,)), ((), ())), preferred_element_type=F32)

    away_parts = [weight_rows(ox, core) for core in range(2)]
    for core in range(2):
        rsend[core * 128 : core * 128 + 128, :] = away_parts[core][:, :128].astype(BF16)
    rsend[256:, :] = jnp.where(low128, away_parts[0][:, 128:], flip(away_parts[1][:, 128:])).astype(BF16)
    weight_out = remote(rsend, rrecv, pair_s.at[3], pair_r.at[3], l_partner)
    weight_out.start()

    loads[3].wait()

    def filter_grad_step(k, carry):
        sums = []
        back = jnp.dot(g_v[k], yb[k], preferred_element_type=F32)
        for l in range(2):
            block = z + 8 * l
            total = carry[l] + ct_v[block, pl.ds(k, 1), :] * back[:128]
            sums.append(total + ct_v[block, pl.ds(k + 16, 1), :] * back[128:])
        return tuple(sums)

    zero = jnp.zeros((128, 128), F32)
    near, far = lax.fori_loop(0, 16, filter_grad_step, (zero, zero), unroll=16)
    own = jnp.where(first, near, far)
    other = jnp.where(first, far, near)
    fsend[...] = jnp.where(low64, other[:64], flip(other[64:]))
    filter_out = remote(fsend, frecv, pair_s.at[4], pair_r.at[4], l_partner)
    filter_out.start()
    fown[...] = own

    for core in range(2):
        rown[core * 128 : core * 128 + 128, :] = weight_rows(xl, core)

    def unfolded(mine, got):
        turned, turned_mine = flip(got), flip(mine)
        low = lax.broadcasted_iota(jnp.int32, mine.shape, 1) < 64
        as_first = jnp.where(low, mine, jnp.concatenate([turned, got], axis=0))
        as_second = jnp.where(low, jnp.concatenate([got, turned], axis=0), turned_mine)
        return jnp.where(first, as_first, as_second)

    weight_out.wait_recv()
    mine = rown[:, :128]
    got = rrecv[:256, :].astype(F32)
    mine_turned, got_turned = flip(mine), flip(got)
    low256 = lax.broadcasted_iota(jnp.int32, (256, 128), 1) < 64
    wg_ref[0] = jnp.where(
        first, jnp.where(low256, mine_turned, got), jnp.where(low256, got_turned, mine)
    )
    wg_ref[1] = jnp.where(
        first, jnp.where(low256, mine, got_turned), jnp.where(low256, got, mine_turned)
    )
    wg_ref[2] = unfolded(rown[:, 128:], rrecv[256:, :].astype(F32))
    filter_out.wait_recv()
    fg_ref[...] = unfolded(fown[...], frecv[...])

    for spread in (tok_a, tok_b, gate_a, gate_b, proj_a, proj_b):
        spread.drain(total)
    for sent in (tok_pair_out, gate_out, proj_out, weight_out, filter_out):
        sent.wait_send()
    for s, rows in ((sib_s, 16 * 128), (tr_s, 7 * 128), (tx_s, 3072), (ts_s, 4096)):
        count(s.at[0], sib_r.at[0], rows).wait_send()


def on_device(tables, tokens, in_weight, filter_taps, grad_out):
    forward, inverse, single = tables
    vmem = pl.BlockSpec(memory_space=pltpu.VMEM)
    anywhere = pl.BlockSpec(memory_space=pltpu.HBM)
    dma = pltpu.SemaphoreType.DMA
    weight_grad, filter_grad = pl.pallas_call(
        kernel,
        out_shape=(
            jax.ShapeDtypeStruct((3, 256, 128), F32),
            jax.ShapeDtypeStruct((128, 128), F32),
        ),
        in_specs=[anywhere] * 7,
        out_specs=(vmem, vmem),
        scratch_shapes=[
            pltpu.VMEM((128, 128), BF16),
            pltpu.VMEM((128, 128), F32),
            pltpu.VMEM((3, 4096, 128), BF16),
            pltpu.VMEM((16, 256, 256), BF16),
            pltpu.VMEM((16, 256, 256), BF16),
            pltpu.VMEM((16, 32, 128), F32),
            pltpu.VMEM((2, 8, 2, 128, 128), BF16),
            pltpu.VMEM((8, 2, 128, 128), BF16),
            pltpu.VMEM((128, 128), BF16),
            pltpu.VMEM((8, 2, 192, 128), BF16),
            pltpu.VMEM((192, 128), BF16),
            pltpu.VMEM((2, 2, 2, 8, 128, 128), BF16),
            pltpu.VMEM((128, 384), F32),
            pltpu.VMEM((16, 128, 128), BF16),
            pltpu.VMEM((16, 256, 128), BF16),
            pltpu.VMEM((16, 256, 128), F32),
            pltpu.VMEM((16, 256, 128), F32),
            pltpu.VMEM((2048, 256), BF16),
            pltpu.VMEM((256, 256), F32),
            pltpu.VMEM((384, 128), BF16),
            pltpu.VMEM((384, 128), BF16),
            pltpu.VMEM((128, 128), F32),
            pltpu.VMEM((64, 128), F32),
            pltpu.VMEM((64, 128), F32),
            dma((7,)),
            dma((6,)),
            *[dma((4,)) for _ in range(6)],
            dma((5,)), dma((5,)),
            dma((1,)), dma((3,)),
            dma((1,)), dma((1,)),
            dma((1,)), dma((2, CHUNKS)), dma((CHUNKS,)),
            dma((1,)), dma((1,)),
        ],
        compiler_params=pltpu.CompilerParams(
            collective_id=0, has_side_effects=True, vmem_limit_bytes=52 * 1024 * 1024
        ),
        cost_estimate=pl.CostEstimate(flops=3_000_000_000, bytes_accessed=10_000_000, transcendentals=0),
    )(
        *[
            pltpu.with_memory_space_constraint(operand, pltpu.HBM)
            for operand in (
                tokens, grad_out, filter_taps, jnp.transpose(in_weight, (1, 0, 2)), forward, inverse, single
            )
        ]
    )
    return jnp.transpose(weight_grad, (1, 0, 2)), filter_grad


def solution(mesh):
    tables = transform_tables()

    def whole(tokens, in_weight, filter_taps, grad_out):
        constants = tuple(jnp.asarray(t) for t in tables)
        placed = (P("ctx", "ch"), P(None, None, "ch"), P("ctx", "ch"), P("ctx", "ch"))
        return jax.shard_map(
            on_device,
            mesh=mesh,
            in_specs=((P(), P(), P()),) + placed,
            out_specs=(P("ctx", None, "ch"), P("ctx", "ch")),
            check_vma=False,
        )(constants, tokens, in_weight, filter_taps, grad_out)

    return whole
```
